128 devices in a mesh: subj: 8 (over y, core), cov: 16 (over x, z).
Axes of the slice: x: 4, y: 4, z: 4, core: 2. Of those that a mesh axis runs over, the one named last changes fastest.
Arguments:
- design: bfloat16 [131072, 4096], P('subj', 'cov'), may hold values from -6 to 6
- coefs: bfloat16 [4096, 32], P('cov'), may hold values from -0.09375 to 0.09375
- penalty: float32 [32], replicated, may hold values from 0.02 to 0.3
- censor: float32 [131072], P('subj'), may hold values from 0.2 to 1
- codes: int32 [131072], P('subj'), may hold values from 0 to 2
- tie_first: int32 [131072], P('subj'), may hold values from 0 to 131071, as said below
- tie_last: int32 [131072], P('subj'), may hold values from 0 to 131071, as said below
Outputs:
- new_coefs: float32 [4096, 32], P('cov')
- weights: float32 [32, 131072], P(None, 'subj')
The draws below stay inside these ranges and needn't reach their ends.
Inputs may be any that keep to these rules, and one draw needn't show every extreme that they name: `tie_first`: tie groups are runs of consecutive subjects; none crosses a multiple of 128. `tie_last`: the last index of the same runs as tie_first.
All inputs are finite; a program needn't handle non-finite values.
Results may differ from the reference program's by a relative error of at most 0.0003.
The reference program's roundings to bfloat16 on the way count: a program that leaves them out, or rounds other values in their place, can miss the bound.
Values sent between devices are 32-bit elements; how exact they have to be, the bound alone decides.
A program may use at most 64 MiB of HBM per device.

```python
import math
import jax
import jax.numpy as jnp
from jax import lax

COVARS = 4096
PATHS = 32
TIE_BLOCK = 128
SUBJECTS = 131072


def tie_groups(key):
    index = jnp.arange(SUBJECTS, dtype=jnp.int32)
    breaks = jax.random.randint(key, (SUBJECTS,), 0, 3) == 0
    breaks = breaks | (index % TIE_BLOCK == 0) | (index == 1) | (index == SUBJECTS - 1)
    first = lax.cummax(jnp.where(breaks, index, 0), axis=0)
    closes = jnp.concatenate([breaks[1:], jnp.ones((1,), dtype=bool)])
    last = lax.cummin(jnp.where(closes, index, SUBJECTS - 1), axis=0, reverse=True)
    return (first.astype(jnp.int32), last.astype(jnp.int32))


def draw_tie_first(key, part):
    return tie_groups(key)[0]


def draw_tie_last(key, part):
    return tie_groups(key)[1]


def plant(drawn, stream_key, smallest, high):
    shape = drawn.shape
    spot = [jax.random.randint(jax.random.fold_in(stream_key, axis), (), 0, shape[axis]) for axis in range(len(shape))]
    drawn = drawn.at[tuple(spot)].set(smallest)
    longest = shape.index(max(shape))
    spot[longest] = (spot[longest] + 1) % shape[longest]
    return drawn.at[tuple(spot)].set(high)


def shard_levels(stream_key, shape, shards, smallest, largest):
    loudness = 1.0
    for dim, shards_of in shards:
        steps = jax.random.uniform(jax.random.fold_in(jax.random.fold_in(stream_key, 6), dim), (shards_of,), jnp.float32, smallest / len(shards), largest / len(shards))
        loudness = loudness * jnp.repeat(jnp.exp(steps), shape[dim] // shards_of).reshape((-1,) + (1,) * (len(shape) - 1 - dim))
    return loudness


def scatter_about(rng, shape, spread, reach, split=(), kind=jnp.bfloat16):
    gain = shard_levels(rng, shape, split, -0.22, 0.18) if split else 1.0
    array = jax.random.normal(rng, shape, jnp.float32) * spread * gain
    return jnp.minimum(jnp.maximum(array, -reach), reach).astype(kind)


def setup_inputs(seed: int = 0) -> dict:
    arg_keys = jax.random.split(jax.random.key(seed), 8)
    return {
        "design": scatter_about(arg_keys[0], (SUBJECTS, COVARS), 1.0, 6.0, ((0, 8), (1, 16))),
        "coefs": scatter_about(arg_keys[1], (COVARS, PATHS), COVARS ** -0.5, 0.09375, ((0, 16),)),
        "penalty": jnp.clip(jnp.exp(jax.random.uniform(arg_keys[2], (PATHS,), jnp.float32, math.log(0.02), math.log(0.3))), 0.02, 0.3),
        "censor": jnp.clip(jnp.exp(math.log(1.0) - 1.609438 * jax.random.uniform(arg_keys[3], (SUBJECTS,), jnp.float32) ** shard_levels(arg_keys[3], (SUBJECTS,), ((0, 8),), -0.2, 0.2)), 0.2, 1.0),
        "codes": plant(jax.random.randint(arg_keys[4], (SUBJECTS,), 0, 3), jax.random.fold_in(arg_keys[4], 1), 0, 2).astype(jnp.int32),
        "tie_first": draw_tie_first(jax.random.fold_in(arg_keys[7], 71), 0),
        "tie_last": draw_tie_last(jax.random.fold_in(arg_keys[7], 71), 0),
    }


def reference(design, coefs, penalty, censor, codes, tie_first, tie_last):
    total_rows = design.shape[0]
    block_rows = min(total_rows, 8192)
    blocks = design.reshape(total_rows // block_rows, block_rows, design.shape[1])
    coefs_wide = coefs.astype(jnp.float32)

    def predict(block):
        return jnp.dot(block.astype(jnp.float32), coefs_wide, precision=lax.Precision.HIGHEST)
    eta = lax.map(predict, blocks).reshape(total_rows, coefs.shape[1]).T
    expo = jnp.exp(eta)
    comp = jnp.where(codes == 2, expo / censor, 0.0)
    comp_before = jnp.cumsum(comp, axis=1) - comp
    risk_after = jnp.flip(jnp.cumsum(jnp.flip(expo, axis=1), axis=1), axis=1)
    risk = risk_after[:, tie_first] + censor * comp_before[:, tie_first]
    inv = jnp.where(codes == 1, 1.0 / risk, 0.0)
    heavy = inv * censor
    inv_upto = jnp.cumsum(inv, axis=1)
    heavy_after = jnp.flip(jnp.cumsum(jnp.flip(heavy, axis=1), axis=1), axis=1) - heavy
    early = inv_upto[:, tie_last]
    later = heavy_after[:, tie_last]
    weights = jnp.where(codes == 1, 1.0, 0.0) - expo * (early + jnp.where(codes == 2, later / censor, 0.0))
    rounded = weights.astype(jnp.bfloat16).astype(jnp.float32)
    rounded_blocks = rounded.reshape(rounded.shape[0], total_rows // block_rows, block_rows).transpose(1, 0, 2)

    def accumulate(total, pair):
        wblock, dblock = pair
        return (total + jnp.dot(wblock, dblock.astype(jnp.float32), precision=lax.Precision.HIGHEST), None)
    start = jnp.zeros((coefs.shape[1], design.shape[1]), jnp.float32)
    score, unused = lax.scan(accumulate, start, (rounded_blocks, blocks))
    shifted = coefs_wide + 0.1 * score.T / jnp.sqrt(jnp.float32(SUBJECTS))
    new_coefs = jnp.sign(shifted) * jnp.maximum(jnp.abs(shifted) - penalty, 0.0)
    return (new_coefs, weights)
```

```python
import functools

import jax
import jax.numpy as jnp
from jax import lax
from jax.experimental import pallas as pl
from jax.experimental.pallas import tpu as pltpu
from jax.sharding import PartitionSpec as P

MESH = pl.DeviceIdType.MESH
F32 = jnp.float32
BF16 = jnp.bfloat16
LANES = 128
SUBJ = 8
RING = 4
PATHS = 32
ROWS = 16384
COLS = 256
BLOCKS = ROWS // LANES
HALF = BLOCKS // 2
QUART = BLOCKS // 4
CHUNK = ROWS // 4
TILE = 1024
NBATCH = 2
COPIES = 128


def split3(x):
    high = x.astype(BF16)
    rest = x - high.astype(F32)
    mid = rest.astype(BF16)
    low = (rest - mid.astype(F32)).astype(BF16)
    return high, mid, low


def dot(a, b):
    return jnp.dot(a, b, preferred_element_type=F32)


def table(kind, wide):
    shape = (LANES, 2 * LANES if wide else LANES)
    row = lax.broadcasted_iota(jnp.int32, shape, 0)
    col = lax.broadcasted_iota(jnp.int32, shape, 1)
    keep = {"ge": row >= col, "lt": row < col, "le": row <= col, "gt": row > col}[kind]
    if wide:
        keep = keep | (col >= LANES)
    return jnp.where(keep, 1.0, 0.0).astype(BF16)


def lane_scan(x, kind):
    wide = table(kind, True)
    high, mid, low = split3(x)
    both = dot(high, wide) + (dot(mid, wide) + dot(low, wide))
    return both[:, :LANES], both[:, LANES:]


def row_scan(totals, kind):
    side = table(kind, False)
    high, mid, low = split3(totals)
    return dot(side, high) + (dot(side, mid) + dot(side, low))


def pick(values, lanes):
    return jnp.take_along_axis(values, lanes, axis=1)


def fold(x):
    return x.reshape(BLOCKS // 8, 8, LANES).sum(axis=0)


def kernel(
    design, coefs, penalty, censor, codes, first, last,
    new_out, weights_out,
    D, C, PEN, CEN, COD, FST, LST, IC2, CT, E, R1, R2, S, R3, R4, ETA, EX, BASE, TS, TR, W, OUTV, SP, SR,
    load_sem, out_sem, send_sem, recv_sem,
):
    s = lax.axis_index("subj")
    cov = lax.axis_index("cov")
    x = cov // RING
    z = cov % RING
    pos = (x, z)

    E5 = E.reshape(RING, RING, 2, BLOCKS, LANES)
    W5 = W.reshape(RING, RING, 2, BLOCKS, LANES)

    def device(axis, at):
        return (s, at * RING + z) if axis == 0 else (s, x * RING + at)

    def ring(axis):
        me = pos[axis]
        return (me + 3) % RING, (me + 1) % RING, (me + 2) % RING

    count = [0]
    started = []

    def send(src, dst, to):
        at = count[0]
        count[0] += 1
        copy = pltpu.make_async_remote_copy(
            src_ref=src, dst_ref=dst, send_sem=send_sem.at[at], recv_sem=recv_sem.at[at],
            device_id=to, device_id_type=MESH,
        )
        copy.start()
        started.append(copy)
        return copy

    loads = []
    for i, (src, dst) in enumerate(
        [(coefs, C), (penalty, PEN), (censor, CEN), (codes, COD), (first, FST), (last, LST)]
    ):
        loads.append(pltpu.make_async_copy(src, dst, load_sem.at[4 + i]))
    order = (0, 2, 1, 3)
    chunks = {}
    for i in order:
        part = pl.ds(i * CHUNK, CHUNK)
        chunks[i] = pltpu.make_async_copy(design.at[part], D.at[part], load_sem.at[i])
    loads[0].start()
    for i in order:
        chunks[i].start()
    for copy in loads[1:]:
        copy.start()

    barrier = pltpu.get_barrier_semaphore()
    peers = [device(axis, at) for axis in (0, 1) for at in ring(axis)[:2]]
    peers += [((s + d) % SUBJ, cov) for d in range(1, SUBJ)]
    for peer in peers:
        pl.semaphore_signal(barrier, inc=1, device_id=peer, device_id_type=MESH)

    loads[0].wait()
    eye = (
        lax.broadcasted_iota(jnp.int32, (PATHS, PATHS), 0)
        == lax.broadcasted_iota(jnp.int32, (PATHS, PATHS), 1)
    )
    nt = (((1,), (1,)), ((), ()))
    CT[...] = lax.dot_general(
        jnp.where(eye, 1.0, 0.0).astype(BF16), C[...], nt, preferred_element_type=F32
    )
    lhs = CT[...].astype(BF16)

    def predict(chunk):
        def body(i, carry):
            start = pl.multiple_of(chunk * CHUNK + i * TILE, TILE)
            part = lax.dot_general(lhs, D[pl.ds(start, TILE), :], nt, preferred_element_type=F32)
            for j in range(TILE // LANES):
                block = chunk * QUART + i * (TILE // LANES) + j
                for g in range(4):
                    E[pl.ds(g * 8 * BLOCKS + block, 8, stride=BLOCKS), :] = part[
                        g * 8 : g * 8 + 8, j * LANES : (j + 1) * LANES
                    ]
            return carry

        lax.fori_loop(0, CHUNK // TILE, body, 0)

    def quarter(ref, half, at, k, start, size):
        rows = pl.ds(half * HALF + start, size)
        return ref.at[at, :, k, rows, :] if half == 0 else ref.at[:, at, k, rows, :]

    sent = {}

    def rs_a(h, k, part):
        left, right, opposite = ring(h)
        start = part * QUART
        near, far = ((left, right) if part == 0 else (right, left))
        d_far, d_near = (0, 1) if part == 0 else (1, 0)
        sent["m1", h, k, d_far] = send(
            quarter(E5, h, opposite, k, start, QUART), R1.at[h, k, d_far], device(h, far)
        )
        sent["m2", h, k, d_near] = send(
            quarter(E5, h, near, k, start, QUART),
            R2.at[h, k, d_near, :, pl.ds(start, QUART), :],
            device(h, near),
        )

    def rs_b(h, k):
        left, right, opposite = ring(h)
        for d, to, start in ((0, right, 0), (1, left, QUART)):
            sent["m1", h, k, d].wait_recv()
            mine = quarter(E5, h, to, k, start, QUART)
            mine[...] = mine[...] + R1[h, k, d]
            sent["m3", h, k, d] = send(
                mine, R2.at[h, k, d, :, pl.ds(start, QUART), :], device(h, to)
            )

    def rs_c(h, k):
        for d in (0, 1):
            sent["m2", h, k, d].wait_recv()
            sent["m3", h, k, d].wait_recv()
        S[h, k] = quarter(E5, h, pos[h], k, 0, HALF)[...] + R2[h, k, 0] + R2[h, k, 1]
        g = 1 - h
        left, right, opposite = ring(g)
        lo, hi = pl.ds(0, QUART), pl.ds(QUART, QUART)
        sent["n1", h, k, 0] = send(S.at[h, k, opposite, lo, :], R3.at[h, k, 0], device(g, right))
        sent["n1", h, k, 1] = send(S.at[h, k, opposite, hi, :], R3.at[h, k, 1], device(g, left))
        sent["n2", h, k, 1] = send(S.at[h, k, left, lo, :], R4.at[h, k, 1, lo, :], device(g, left))
        sent["n2", h, k, 0] = send(S.at[h, k, right, hi, :], R4.at[h, k, 0, hi, :], device(g, right))

    def rs_d(h, k):
        g = 1 - h
        left, right, opposite = ring(g)
        for d, to, start in ((0, right, 0), (1, left, QUART)):
            sent["n1", h, k, d].wait_recv()
            mine = S.at[h, k, to, pl.ds(start, QUART), :]
            mine[...] = mine[...] + R3[h, k, d]
            sent["n3", h, k, d] = send(
                mine, R4.at[h, k, d, pl.ds(start, QUART), :], device(g, to)
            )

    def rs_e(h, k):
        for d in (0, 1):
            sent["n2", h, k, d].wait_recv()
            sent["n3", h, k, d].wait_recv()
        ETA[k, pl.ds(h * HALF, HALF), :] = S[h, k, pos[1 - h]] + R4[h, k, 0] + R4[h, k, 1]

    def exchange(k, e):
        for d in range(1, SUBJ):
            sent["t", k, e, d] = send(TS.at[k, e], TR.at[k, e, d], ((s + d) % SUBJ, cov))

    def arrived(k, e):
        after = jnp.zeros((8, LANES), F32)
        before = jnp.zeros((8, LANES), F32)
        for d in range(1, SUBJ):
            sent["t", k, e, d].wait_recv()
            after = after + jnp.where(d > s, TR[k, e, d, 0], 0.0)
            before = before + jnp.where(d <= s, TR[k, e, d, 1], 0.0)
        return jnp.sum(after, keepdims=True), jnp.sum(before, keepdims=True)

    def prepare():
        for copy in loads[1:]:
            copy.wait()
        FST[...] = FST[...] & (LANES - 1)
        LST[...] = LST[...] & (LANES - 1)
        IC2[...] = jnp.where(COD[...] == 2, 1.0 / CEN[...], 0.0)

    def scan_a(k):
        expo = jnp.exp(ETA[k])
        comp = expo * IC2[...]
        EX[k] = expo
        TS[k, 0, 0] = fold(expo)
        TS[k, 0, 1] = fold(comp)
        exchange(k, 0)
        risk, risk_rows = lane_scan(expo, "ge")
        before, before_rows = lane_scan(comp, "lt")
        lanes = FST[...]
        BASE[k] = (pick(risk, lanes) + row_scan(risk_rows, "lt")) + CEN[...] * (
            pick(before, lanes) + row_scan(before_rows, "gt")
        )

    def scan_b(k):
        risk_in, comp_in = arrived(k, 0)
        risk = BASE[k] + (risk_in + CEN[...] * comp_in)
        inv = jnp.where(COD[...] == 1, 1.0 / risk, 0.0)
        heavy = inv * CEN[...]
        TS[k, 1, 0] = fold(heavy)
        TS[k, 1, 1] = fold(inv)
        exchange(k, 1)
        upto, upto_rows = lane_scan(inv, "le")
        later, later_rows = lane_scan(heavy, "gt")
        lanes = LST[...]
        BASE[k] = (pick(upto, lanes) + row_scan(upto_rows, "gt")) + IC2[...] * (
            pick(later, lanes) + row_scan(later_rows, "lt")
        )

    def scan_c(k):
        later_in, early_in = arrived(k, 1)
        event = jnp.where(COD[...] == 1, 1.0, 0.0)
        W5[x, z, k] = event - EX[k] * (BASE[k] + (early_in + IC2[...] * later_in))

    def spot(h, k, axis, at, start, size):
        rows = pl.ds(h * HALF + start, size)
        if axis == 0:
            return W5.at[at, z, k, rows, :]
        return W5.at[x, at, k, rows, :]

    def ag_a(h, k):
        g = 1 - h
        left, right, opposite = ring(g)
        mine = spot(h, k, g, pos[g], 0, HALF)
        sent["a1", h, k, 0] = send(mine, mine, device(g, right))
        sent["a1", h, k, 1] = send(mine, mine, device(g, left))

    def ag_b(h, k):
        g = 1 - h
        left, right, opposite = ring(g)
        for d, came, to, start in ((0, left, right, 0), (1, right, left, QUART)):
            sent["a1", h, k, d].wait_recv()
            piece = spot(h, k, g, came, start, QUART)
            sent["a2", h, k, d] = send(piece, piece, device(g, to))

    def ag_c(h, k):
        left, right, opposite = ring(h)
        for d in (0, 1):
            sent["a2", h, k, d].wait_recv()
        mine = quarter(W5, h, pos[h], k, 0, HALF)
        sent["a3", h, k, 0] = send(mine, mine, device(h, right))
        sent["a3", h, k, 1] = send(mine, mine, device(h, left))

    def ag_d(h, k):
        left, right, opposite = ring(h)
        for d, came, to, start in ((0, left, right, 0), (1, right, left, QUART)):
            sent["a3", h, k, d].wait_recv()
            piece = quarter(W5, h, came, k, start, QUART)
            sent["a4", h, k, d] = send(piece, piece, device(h, to))

    def ag_e(h, k):
        for d in (0, 1):
            sent["a4", h, k, d].wait_recv()

    for i, (chunk, h, part) in enumerate(((0, 0, 0), (2, 1, 0), (1, 0, 1), (3, 1, 1))):
        chunks[chunk].wait()
        predict(chunk)
        if i == 0:
            pl.semaphore_wait(barrier, len(peers))
        rs_a(h, 0, part)
    both = (0, 1)
    for h in both:
        rs_b(h, 0)
    for h in both:
        rs_a(h, 1, 0)
        rs_a(h, 1, 1)
    prepare()
    for h in both:
        rs_c(h, 0)
    for h in both:
        rs_d(h, 0)
    for h in both:
        rs_b(h, 1)
    for h in both:
        rs_e(h, 0)
    scan_a(0)
    for h in both:
        rs_c(h, 1)
    scan_b(0)
    for h in both:
        rs_d(h, 1)
    for h in both:
        rs_e(h, 1)
    scan_a(1)
    scan_c(0)
    for h in both:
        ag_a(h, 0)
    scan_b(1)
    for h in both:
        ag_b(h, 0)
    for h in both:
        ag_c(h, 0)
    scan_c(1)
    for h in both:
        ag_a(h, 1)
    for h in both:
        ag_b(h, 1)
    for h in both:
        ag_d(h, 0)
    for h in both:
        ag_c(h, 1)
    for h in both:
        ag_e(h, 0)
    for h in both:
        ag_d(h, 1)
    for h in both:
        ag_e(h, 1)

    def accumulate(i, total):
        start = pl.multiple_of(i * TILE, TILE)
        parts = []
        for j in range(TILE // LANES):
            block = i * (TILE // LANES) + j
            parts.append(
                jnp.concatenate(
                    [W[pl.ds(g * 8 * BLOCKS + block, 8, stride=BLOCKS), :] for g in range(4)], axis=0
                )
            )
        tile = jnp.concatenate(parts, axis=1)
        OUTV[:, pl.ds(start, TILE)] = tile
        return total + dot(tile.astype(BF16), D[pl.ds(start, TILE), :])

    total = jnp.zeros((PATHS, COLS), F32)
    outs = []
    for c in range(4):
        total = lax.fori_loop(c * (CHUNK // TILE), (c + 1) * (CHUNK // TILE), accumulate, total)
        part = pl.ds(c * CHUNK, CHUNK)
        copy = pltpu.make_async_copy(OUTV.at[:, part], weights_out.at[:, part], out_sem.at[c])
        copy.start()
        outs.append(copy)
    SP[...] = total
    for d in range(1, SUBJ):
        sent["s", d] = send(SP, SR.at[s], ((s + d) % SUBJ, cov))
    SR[s] = total
    for d in range(1, SUBJ):
        sent["s", d].wait_recv()
    score = SR[0]
    for i in range(1, SUBJ):
        score = score + SR[i]
    scale = 0.1 / jnp.sqrt(F32(SUBJ * ROWS))
    limit = jnp.sum(jnp.where(eye, jnp.broadcast_to(PEN[...], (PATHS, PATHS)), 0.0), axis=1, keepdims=True)
    shifted = CT[...] + scale * score
    sign = jnp.where(shifted > 0, 1.0, jnp.where(shifted < 0, -1.0, 0.0))
    new_out[...] = sign * jnp.maximum(jnp.abs(shifted) - limit, 0.0)
    for copy in outs:
        copy.wait()
    for copy in started:
        copy.wait_send()


def local(design, coefs, penalty, censor, codes, tie_first, tie_last):
    square = (BLOCKS, LANES)
    anywhere = pl.BlockSpec(memory_space=pl.ANY)
    vmem = pltpu.VMEM
    dma = pltpu.SemaphoreType.DMA
    new, weights = pl.pallas_call(
        kernel,
        out_shape=(
            jax.ShapeDtypeStruct((PATHS, COLS), F32),
            jax.ShapeDtypeStruct((PATHS, ROWS), F32),
        ),
        in_specs=[anywhere] * 7,
        out_specs=(pl.BlockSpec(memory_space=pltpu.VMEM), anywhere),
        scratch_shapes=[
            vmem((ROWS, COLS), BF16),
            vmem((COLS, PATHS), BF16),
            vmem((1, PATHS), F32),
            vmem(square, F32),
            vmem(square, jnp.int32),
            vmem(square, jnp.int32),
            vmem(square, jnp.int32),
            vmem(square, F32),
            vmem((PATHS, COLS), F32),
            vmem((PATHS * BLOCKS, LANES), F32),
            vmem((2, NBATCH, 2, RING, QUART, LANES), F32),
            vmem((2, NBATCH, 2, RING, HALF, LANES), F32),
            vmem((2, NBATCH, RING, HALF, LANES), F32),
            vmem((2, NBATCH, 2, QUART, LANES), F32),
            vmem((2, NBATCH, 2, HALF, LANES), F32),
            vmem((NBATCH, BLOCKS, LANES), F32),
            vmem((NBATCH, BLOCKS, LANES), F32),
            vmem((NBATCH, BLOCKS, LANES), F32),
            vmem((NBATCH, 2, 2, 8, LANES), F32),
            vmem((NBATCH, 2, SUBJ, 2, 8, LANES), F32),
            vmem((PATHS * BLOCKS, LANES), F32),
            vmem((PATHS, ROWS), F32),
            vmem((PATHS, COLS), F32),
            vmem((SUBJ, PATHS, COLS), F32),
            dma((10,)),
            dma((4,)),
            dma((COPIES,)),
            dma((COPIES,)),
        ],
        compiler_params=pltpu.CompilerParams(
            collective_id=0, has_side_effects=True, vmem_limit_bytes=48 * 2**20
        ),
        cost_estimate=pl.CostEstimate(
            flops=4 * PATHS * ROWS * COLS,
            bytes_accessed=2 * ROWS * COLS + 4 * PATHS * ROWS,
            transcendentals=2 * ROWS,
        ),
    )(
        design,
        coefs,
        penalty.reshape(1, PATHS),
        censor.reshape(square),
        codes.reshape(square),
        tie_first.reshape(square),
        tie_last.reshape(square),
    )
    return new.T, weights


def solution(mesh):
    in_specs = (P("subj", "cov"), P("cov", None), P(), P("subj"), P("subj"), P("subj"), P("subj"))
    out_specs = (P("cov", None), P(None, "subj"))
    return jax.shard_map(local, mesh=mesh, in_specs=in_specs, out_specs=out_specs, check_vma=False)
```

```python
import functools

import jax
import jax.numpy as jnp
from jax import lax
from jax.experimental import pallas as pl
from jax.experimental.pallas import tpu as pltpu
from jax.sharding import PartitionSpec as P

MESH = pl.DeviceIdType.MESH
F32 = jnp.float32
BF16 = jnp.bfloat16
LANES = 128
SUBJ = 8
RING = 4
PATHS = 32
ROWS = 16384
COLS = 256
BLOCKS = ROWS // LANES
HALF = BLOCKS // 2
QUART = BLOCKS // 4
CHUNK = ROWS // 4
TILE1 = 4096
TILE2 = 4096
NBATCH = 2


def split3(x):
    high = x.astype(BF16)
    rest = x - high.astype(F32)
    mid = rest.astype(BF16)
    low = (rest - mid.astype(F32)).astype(BF16)
    return high, mid, low


def dot(a, b):
    return jnp.dot(a, b, preferred_element_type=F32)


def table(kind, wide):
    shape = (LANES, 2 * LANES if wide else LANES)
    row = lax.broadcasted_iota(jnp.int32, shape, 0)
    col = lax.broadcasted_iota(jnp.int32, shape, 1)
    keep = {"ge": row >= col, "lt": row < col, "le": row <= col, "gt": row > col}[kind]
    if wide:
        keep = keep | (col >= LANES)
    return jnp.where(keep, 1.0, 0.0).astype(BF16)


def lane_scan(x, kind):
    wide = table(kind, True)
    high, mid, low = split3(x)
    both = dot(high, wide) + (dot(mid, wide) + dot(low, wide))
    return both[:, :LANES], both[:, LANES:]


def row_scan(totals, kind):
    side = table(kind, False)
    high, mid, low = split3(totals)
    return dot(side, high) + (dot(side, mid) + dot(side, low))


def pick(values, lanes):
    return jnp.take_along_axis(values, lanes, axis=1)


def fold(x):
    return x.reshape(BLOCKS // 8, 8, LANES).sum(axis=0)


def kernel(
    design, coefs, penalty, censor, codes, first, last,
    new_out, weights_out,
    D, C, PEN, CEN, COD, FST, LST, IC2, E, R1, R2, S, R4, ETA, EX, BASE, TS, TR, W, SP, SR, SUM,
    load_sem, send_sem, recv_sem,
):
    s = lax.axis_index("subj")
    cov = lax.axis_index("cov")
    x = cov // RING
    z = cov % RING
    pos = (x, z)

    E5 = E.reshape(RING, RING, 2, BLOCKS, LANES)
    W5 = W.reshape(RING, RING, 2, BLOCKS, LANES)

    def device(axis, at):
        return (s, at * RING + z) if axis == 0 else (s, x * RING + at)

    def ring(axis):
        me = pos[axis]
        return (me + 3) % RING, (me + 1) % RING, (me + 2) % RING

    sent_rows = [0]
    groups = {}

    def rows_of(ref):
        size = 1
        for n in ref.shape[:-1]:
            size *= n
        return size * ref.shape[-1] // LANES

    def send(group, src, dst, to):
        at, rows = groups.get(group, (len(groups), 0))
        groups[group] = (at, rows + rows_of(src))
        sent_rows[0] += rows_of(src)
        pltpu.make_async_remote_copy(
            src_ref=src, dst_ref=dst, send_sem=send_sem.at[0], recv_sem=recv_sem.at[at],
            device_id=to, device_id_type=MESH,
        ).start()

    def wait_rows(sem, rows):
        span = W.at[pl.ds(0, rows), :] if rows <= PATHS * BLOCKS else None
        pltpu.make_async_copy(span, span, sem).wait()

    def received(*group):
        at, rows = groups[group]
        wait_rows(recv_sem.at[at], rows)

    order = (0, 2, 1, 3)
    chunks = {}
    for i in order:
        part = pl.ds(i * CHUNK, CHUNK)
        chunks[i] = pltpu.make_async_copy(design.at[part], D.at[part], load_sem.at[i])
    small = []
    for i, (src, dst) in enumerate(
        [(coefs, C), (penalty, PEN), (censor, CEN), (codes, COD), (first, FST), (last, LST)]
    ):
        small.append(pltpu.make_async_copy(src, dst, load_sem.at[4 + i]))
    small[0].start()
    for i in order:
        chunks[i].start()
    for copy in small[1:]:
        copy.start()

    barrier = pltpu.get_barrier_semaphore()
    peers = [device(axis, at) for axis in (0, 1) for at in ring(axis)]
    peers += [((s + d) % SUBJ, cov) for d in range(1, SUBJ)]
    for peer in peers:
        pl.semaphore_signal(barrier, inc=1, device_id=peer, device_id_type=MESH)

    small[0].wait()
    nt = (((1,), (1,)), ((), ()))
    lhs = C[...]

    def predict(chunk):
        for i in range(CHUNK // TILE1):
            start = chunk * CHUNK + i * TILE1
            part = lax.dot_general(lhs, D[start : start + TILE1, :], nt, preferred_element_type=F32)
            for j in range(TILE1 // LANES):
                block = start // LANES + j
                for g in range(4):
                    E[pl.ds(g * 8 * BLOCKS + block, 8, stride=BLOCKS), :] = part[
                        g * 8 : g * 8 + 8, j * LANES : (j + 1) * LANES
                    ]

    def quarter(ref, half, at, k, start, size):
        rows = pl.ds(half * HALF + start, size)
        return ref.at[at, :, k, rows, :] if half == 0 else ref.at[:, at, k, rows, :]

    def rs_far(h, k, part):
        left, right, opposite = ring(h)
        start, d, to = ((0, 0, right), (QUART, 1, left))[part]
        send(("m1", h, k), quarter(E5, h, opposite, k, start, QUART), R1.at[h, k, d], device(h, to))

    def rs_near(h, k, part):
        left, right, opposite = ring(h)
        start, d, to = ((0, 1, left), (QUART, 0, right))[part]
        send(
            ("m2", h, k),
            quarter(E5, h, to, k, start, QUART),
            R2.at[h, k, d, :, pl.ds(start, QUART), :],
            device(h, to),
        )

    def rs_on(h, k):
        left, right, opposite = ring(h)
        received("m1", h, k)
        for d, to, start in ((0, right, 0), (1, left, QUART)):
            mine = quarter(E5, h, to, k, start, QUART)
            mine[...] = mine[...] + R1[h, k, d]
            send(("m2", h, k), mine, R2.at[h, k, d, :, pl.ds(start, QUART), :], device(h, to))

    def rs_second(h, k):
        received("m2", h, k)
        S[h, k] = quarter(E5, h, pos[h], k, 0, HALF)[...] + R2[h, k, 0] + R2[h, k, 1]
        for slot, at in enumerate(ring(1 - h)):
            send(("n", h, k), S.at[h, k, at], R4.at[h, k, slot], device(1 - h, at))

    def rs_end(h, k):
        received("n", h, k)
        ETA[k, pl.ds(h * HALF, HALF), :] = S[h, k, pos[1 - h]] + (
            R4[h, k, 0] + R4[h, k, 1] + R4[h, k, 2]
        )

    def exchange(k, e):
        for d in range(1, SUBJ):
            send(("t", k, e), TS.at[k, e], TR.at[k, e, d], ((s + d) % SUBJ, cov))

    def arrived(k, e):
        received("t", k, e)
        after = jnp.zeros((8, LANES), F32)
        before = jnp.zeros((8, LANES), F32)
        for d in range(1, SUBJ):
            after = after + jnp.where(d > s, TR[k, e, d, 0], 0.0)
            before = before + jnp.where(d <= s, TR[k, e, d, 1], 0.0)
        return jnp.sum(after, keepdims=True), jnp.sum(before, keepdims=True)

    def prepare():
        for copy in small[1:]:
            copy.wait()
        FST[...] = FST[...] & (LANES - 1)
        LST[...] = LST[...] & (LANES - 1)
        IC2[...] = jnp.where(COD[...] == 2, 1.0 / CEN[...], 0.0)

    def scan_a(k):
        expo = jnp.exp(ETA[k])
        comp = expo * IC2[...]
        EX[k] = expo
        TS[k, 0, 0] = fold(expo)
        TS[k, 0, 1] = fold(comp)
        exchange(k, 0)
        risk, risk_rows = lane_scan(expo, "ge")
        before, before_rows = lane_scan(comp, "lt")
        lanes = FST[...]
        BASE[k] = (pick(risk, lanes) + row_scan(risk_rows, "lt")) + CEN[...] * (
            pick(before, lanes) + row_scan(before_rows, "gt")
        )

    def scan_b(k):
        risk_in, comp_in = arrived(k, 0)
        risk = BASE[k] + (risk_in + CEN[...] * comp_in)
        inv = jnp.where(COD[...] == 1, 1.0 / risk, 0.0)
        heavy = inv * CEN[...]
        TS[k, 1, 0] = fold(heavy)
        TS[k, 1, 1] = fold(inv)
        exchange(k, 1)
        upto, upto_rows = lane_scan(inv, "le")
        later, later_rows = lane_scan(heavy, "gt")
        lanes = LST[...]
        BASE[k] = (pick(upto, lanes) + row_scan(upto_rows, "gt")) + IC2[...] * (
            pick(later, lanes) + row_scan(later_rows, "lt")
        )

    def scan_c(k):
        later_in, early_in = arrived(k, 1)
        event = jnp.where(COD[...] == 1, 1.0, 0.0)
        W5[x, z, k] = event - EX[k] * (BASE[k] + (early_in + IC2[...] * later_in))

    def spot(h, k, at):
        rows = pl.ds(h * HALF, HALF)
        return W5.at[x, at, k, rows, :] if h == 0 else W5.at[at, z, k, rows, :]

    def ag_first(h, k):
        mine = spot(h, k, pos[1 - h])
        for at in ring(1 - h):
            send(("a1", h, k), mine, mine, device(1 - h, at))
        for at in ring(h):
            send(("a2", h, k), mine, mine, device(h, at))

    def ag_second(h, k):
        received("a1", h, k)
        for came in ring(1 - h):
            piece = spot(h, k, came)
            for at in ring(h):
                send(("a2", h, k), piece, piece, device(h, at))

    def ag_end(h, k):
        received("a2", h, k)

    def score(k):
        total = jnp.zeros((PATHS // 2, COLS), F32)
        for i in range(ROWS // TILE2):
            start = i * TILE2
            parts = []
            for j in range(TILE2 // LANES):
                block = start // LANES + j
                rows = [
                    W[pl.ds((g * 16 + k) * BLOCKS + block, 8, stride=2 * BLOCKS), :]
                    for g in range(2)
                ]
                parts.append(jnp.concatenate(rows, axis=0).astype(BF16))
            total = total + dot(jnp.concatenate(parts, axis=1), D[start : start + TILE2, :])
        SP[k] = total
        for d in range(1, SUBJ):
            send(("s", k), SP.at[k], SR.at[k, s], ((s + d) % SUBJ, cov))
        SR[k, s] = total

    both = (0, 1)
    for i, (chunk, h, part) in enumerate(((0, 0, 0), (2, 1, 0), (1, 0, 1), (3, 1, 1))):
        chunks[chunk].wait()
        predict(chunk)
        if i == 0:
            pl.semaphore_wait(barrier, len(peers))
        rs_far(h, 0, part)
        rs_near(h, 0, part)
    for h in both:
        rs_far(h, 1, 0)
        rs_far(h, 1, 1)
    for h in both:
        rs_on(h, 0)
    for h in both:
        rs_near(h, 1, 0)
        rs_near(h, 1, 1)
    prepare()
    for h in both:
        rs_on(h, 1)
    for k in both:
        for h in both:
            rs_second(h, k)
    for h in both:
        rs_end(h, 0)
    scan_a(0)
    for h in both:
        rs_end(h, 1)
    scan_a(1)
    for k in both:
        scan_b(k)
    for k in both:
        scan_c(k)
        for h in both:
            ag_first(h, k)
    for k in both:
        for h in both:
            ag_second(h, k)
    for h in both:
        ag_end(h, 0)
    score(0)
    for h in both:
        ag_end(h, 1)
    score(1)

    for block in range(BLOCKS):
        for g in range(4):
            weights_out[g * 8 : g * 8 + 8, block * LANES : (block + 1) * LANES] = W[
                pl.ds(g * 8 * BLOCKS + block, 8, stride=BLOCKS), :
            ]
    eye = (
        lax.broadcasted_iota(jnp.int32, (PATHS, PATHS), 0)
        == lax.broadcasted_iota(jnp.int32, (PATHS, PATHS), 1)
    )
    limit = jnp.sum(
        jnp.where(eye, jnp.broadcast_to(PEN[...], (PATHS, PATHS)), 0.0), axis=1, keepdims=True
    )
    wide = C[...].astype(F32)
    for k in both:
        received("s", k)
        total = SR[k, 0]
        for i in range(1, SUBJ):
            total = total + SR[k, i]
        for c in range(2):
            SUM[c, pl.ds(k, PATHS // 2, stride=2), :] = total[:, c * LANES : (c + 1) * LANES]
    scale = 0.1 / jnp.sqrt(F32(SUBJ * ROWS))
    for c in range(2):
        cols = slice(c * LANES, (c + 1) * LANES)
        shifted = wide[:, cols] + scale * SUM[c]
        sign = jnp.where(shifted > 0, 1.0, jnp.where(shifted < 0, -1.0, 0.0))
        new_out[:, cols] = sign * jnp.maximum(jnp.abs(shifted) - limit, 0.0)
    left_rows = sent_rows[0]
    span = D.at[pl.ds(0, left_rows), :]
    pltpu.make_async_copy(span, span, send_sem.at[0]).wait()


def local(design, coefs, penalty, censor, codes, tie_first, tie_last):
    square = (BLOCKS, LANES)
    vmem = pltpu.VMEM
    dma = pltpu.SemaphoreType.DMA
    new, weights = pl.pallas_call(
        kernel,
        out_shape=(
            jax.ShapeDtypeStruct((PATHS, COLS), F32),
            jax.ShapeDtypeStruct((PATHS, ROWS), F32),
        ),
        in_specs=[pl.BlockSpec(memory_space=pltpu.HBM)] * 7,
        out_specs=(pl.BlockSpec(memory_space=pltpu.VMEM), pl.BlockSpec(memory_space=pltpu.VMEM)),
        scratch_shapes=[
            vmem((ROWS, COLS), BF16),
            vmem((PATHS, COLS), BF16),
            vmem((1, PATHS), F32),
            vmem(square, F32),
            vmem(square, jnp.int32),
            vmem(square, jnp.int32),
            vmem(square, jnp.int32),
            vmem(square, F32),
            vmem((PATHS * BLOCKS, LANES), F32),
            vmem((2, NBATCH, 2, RING, QUART, LANES), F32),
            vmem((2, NBATCH, 2, RING, HALF, LANES), F32),
            vmem((2, NBATCH, RING, HALF, LANES), F32),
            vmem((2, NBATCH, 3, HALF, LANES), F32),
            vmem((NBATCH, BLOCKS, LANES), F32),
            vmem((NBATCH, BLOCKS, LANES), F32),
            vmem((NBATCH, BLOCKS, LANES), F32),
            vmem((NBATCH, 2, 2, 8, LANES), F32),
            vmem((NBATCH, 2, SUBJ, 2, 8, LANES), F32),
            vmem((PATHS * BLOCKS, LANES), F32),
            vmem((NBATCH, PATHS // 2, COLS), F32),
            vmem((NBATCH, SUBJ, PATHS // 2, COLS), F32),
            vmem((2, PATHS, LANES), F32),
            dma((10,)),
            dma((1,)),
            dma((26,)),
        ],
        compiler_params=pltpu.CompilerParams(
            collective_id=0, has_side_effects=True, vmem_limit_bytes=48 * 2**20
        ),
        cost_estimate=pl.CostEstimate(
            flops=4 * PATHS * ROWS * COLS,
            bytes_accessed=2 * ROWS * COLS + 4 * PATHS * ROWS,
            transcendentals=2 * ROWS,
        ),
    )(
        design,
        coefs.T,
        penalty.reshape(1, PATHS),
        censor.reshape(square),
        codes.reshape(square),
        tie_first.reshape(square),
        tie_last.reshape(square),
    )
    return new.T, weights


def solution(mesh):
    in_specs = (P("subj", "cov"), P("cov", None), P(), P("subj"), P("subj"), P("subj"), P("subj"))
    out_specs = (P("cov", None), P(None, "subj"))
    return jax.shard_map(local, mesh=mesh, in_specs=in_specs, out_specs=out_specs, check_vma=False)
```

```python
import functools

import jax
import jax.numpy as jnp
from jax import lax
from jax.experimental import pallas as pl
from jax.experimental.pallas import tpu as pltpu
from jax.sharding import PartitionSpec as P

MESH = pl.DeviceIdType.MESH
F32 = jnp.float32
BF16 = jnp.bfloat16
LANES = 128
SUBJ = 8
RING = 4
PATHS = 32
ROWS = 16384
COLS = 256
BLOCKS = ROWS // LANES
HALF = BLOCKS // 2
QUART = BLOCKS // 4
CHUNK = ROWS // 4
TILE1 = 4096
NBATCH = 2


def split3(x):
    high = x.astype(BF16)
    rest = x - high.astype(F32)
    mid = rest.astype(BF16)
    low = (rest - mid.astype(F32)).astype(BF16)
    return high, mid, low


def dot(a, b):
    return jnp.dot(a, b, preferred_element_type=F32)


def table(kind, wide):
    shape = (LANES, 2 * LANES if wide else LANES)
    row = lax.broadcasted_iota(jnp.int32, shape, 0)
    col = lax.broadcasted_iota(jnp.int32, shape, 1)
    keep = {"ge": row >= col, "lt": row < col, "le": row <= col, "gt": row > col}[kind]
    if wide:
        keep = keep | (col >= LANES)
    return jnp.where(keep, 1.0, 0.0).astype(BF16)


def lane_scan(x, kind):
    wide = table(kind, True)
    high, mid, low = split3(x)
    both = dot(high, wide) + (dot(mid, wide) + dot(low, wide))
    return both[:, :LANES], both[:, LANES:]


def row_scan(totals, kind):
    side = table(kind, False)
    high, mid, low = split3(totals)
    return dot(side, high) + (dot(side, mid) + dot(side, low))


def pick(values, lanes):
    return jnp.take_along_axis(values, lanes, axis=1)


def fold(x):
    return x.reshape(BLOCKS // 8, 8, LANES).sum(axis=0)


def kernel(
    design, coefs, penalty, censor, codes, first, last,
    new_out, weights_out,
    D, C, PEN, CEN, COD, FST, LST, IC2, E, R1, R2, S, R4, ETA, EX, BASE, TS, TR, W, SP, SR, SUM, OUTV,
    load_sem, out_sem, send_sem, recv_sem,
):
    s = lax.axis_index("subj")
    cov = lax.axis_index("cov")
    x = cov // RING
    z = cov % RING
    pos = (x, z)

    E5 = E.reshape(RING, RING, 2, BLOCKS, LANES)
    W5 = W.reshape(RING, RING, 2, BLOCKS, LANES)

    def device(axis, at):
        return (s, at * RING + z) if axis == 0 else (s, x * RING + at)

    def ring(axis):
        me = pos[axis]
        return (me + 3) % RING, (me + 1) % RING, (me + 2) % RING

    sent_rows = [0]
    groups = {}

    def rows_of(ref):
        size = 1
        for n in ref.shape[:-1]:
            size *= n
        return size * ref.shape[-1] // LANES

    def send(group, src, dst, to):
        at, rows = groups.get(group, (len(groups), 0))
        groups[group] = (at, rows + rows_of(src))
        sent_rows[0] += rows_of(src)
        pltpu.make_async_remote_copy(
            src_ref=src, dst_ref=dst, send_sem=send_sem.at[0], recv_sem=recv_sem.at[at],
            device_id=to, device_id_type=MESH,
        ).start()

    def wait_rows(sem, rows):
        span = W.at[pl.ds(0, rows), :] if rows <= PATHS * BLOCKS else None
        pltpu.make_async_copy(span, span, sem).wait()

    def received(*group):
        at, rows = groups[group]
        wait_rows(recv_sem.at[at], rows)

    barrier = pltpu.get_barrier_semaphore()
    peers = [device(axis, at) for axis in (0, 1) for at in ring(axis)]
    peers += [((s + d) % SUBJ, cov) for d in range(1, SUBJ)]
    for peer in peers:
        pl.semaphore_signal(barrier, inc=1, device_id=peer, device_id_type=MESH)

    order = (0, 2, 1, 3)
    chunks = {}
    for i in order:
        part = pl.ds(i * CHUNK, CHUNK)
        chunks[i] = pltpu.make_async_copy(design.at[part], D.at[part], load_sem.at[i])
    small = []
    for i, (src, dst) in enumerate(
        [(coefs, C), (penalty, PEN), (censor, CEN), (codes, COD), (first, FST), (last, LST)]
    ):
        small.append(pltpu.make_async_copy(src, dst, load_sem.at[4 + i]))
    small[0].start()
    for i in order:
        chunks[i].start()
    for copy in small[1:]:
        copy.start()

    small[0].wait()
    nt = (((1,), (1,)), ((), ()))
    lhs = C[...]

    def predict(chunk):
        for i in range(CHUNK // TILE1):
            start = chunk * CHUNK + i * TILE1
            part = lax.dot_general(lhs, D[start : start + TILE1, :], nt, preferred_element_type=F32)
            for j in range(TILE1 // LANES):
                block = start // LANES + j
                for g in range(4):
                    E[pl.ds(g * 8 * BLOCKS + block, 8, stride=BLOCKS), :] = part[
                        g * 8 : g * 8 + 8, j * LANES : (j + 1) * LANES
                    ]

    def quarter(ref, half, at, k, start, size):
        rows = pl.ds(half * HALF + start, size)
        return ref.at[at, :, k, rows, :] if half == 0 else ref.at[:, at, k, rows, :]

    def rs_far(h, k, part):
        left, right, opposite = ring(h)
        start, d, to = ((0, 0, right), (QUART, 1, left))[part]
        send(("m1", h, k), quarter(E5, h, opposite, k, start, QUART), R1.at[h, k, d], device(h, to))

    def rs_near(h, k, part):
        left, right, opposite = ring(h)
        start, d, to = ((0, 1, left), (QUART, 0, right))[part]
        send(
            ("m2", h, k),
            quarter(E5, h, to, k, start, QUART),
            R2.at[h, k, d, :, pl.ds(start, QUART), :],
            device(h, to),
        )

    def rs_on(h, k):
        left, right, opposite = ring(h)
        received("m1", h, k)
        for d, to, start in ((0, right, 0), (1, left, QUART)):
            mine = quarter(E5, h, to, k, start, QUART)
            mine[...] = mine[...] + R1[h, k, d]
            send(("m2", h, k), mine, R2.at[h, k, d, :, pl.ds(start, QUART), :], device(h, to))

    def rs_second(h, k):
        received("m2", h, k)
        S[h, k] = quarter(E5, h, pos[h], k, 0, HALF)[...] + R2[h, k, 0] + R2[h, k, 1]
        for slot, at in enumerate(ring(1 - h)):
            send(("n", h, k), S.at[h, k, at], R4.at[h, k, slot], device(1 - h, at))

    def rs_end(h, k):
        received("n", h, k)
        ETA[k, pl.ds(h * HALF, HALF), :] = S[h, k, pos[1 - h]] + (
            R4[h, k, 0] + R4[h, k, 1] + R4[h, k, 2]
        )

    def exchange(k, e):
        for d in range(1, SUBJ):
            send(("t", k, e), TS.at[k, e], TR.at[k, e, d], ((s + d) % SUBJ, cov))

    def arrived(k, e):
        received("t", k, e)
        after = jnp.zeros((8, LANES), F32)
        before = jnp.zeros((8, LANES), F32)
        for d in range(1, SUBJ):
            after = after + jnp.where(d > s, TR[k, e, d, 0], 0.0)
            before = before + jnp.where(d <= s, TR[k, e, d, 1], 0.0)
        return jnp.sum(after, keepdims=True), jnp.sum(before, keepdims=True)

    def prepare():
        for copy in small[1:]:
            copy.wait()
        FST[...] = FST[...] & (LANES - 1)
        LST[...] = LST[...] & (LANES - 1)
        IC2[...] = jnp.where(COD[...] == 2, 1.0 / CEN[...], 0.0)

    def scan_a(k):
        expo = jnp.exp(ETA[k])
        comp = expo * IC2[...]
        EX[k] = expo
        TS[k, 0, 0] = fold(expo)
        TS[k, 0, 1] = fold(comp)
        exchange(k, 0)
        risk, risk_rows = lane_scan(expo, "ge")
        before, before_rows = lane_scan(comp, "lt")
        lanes = FST[...]
        BASE[k] = (pick(risk, lanes) + row_scan(risk_rows, "lt")) + CEN[...] * (
            pick(before, lanes) + row_scan(before_rows, "gt")
        )

    def scan_b(k):
        risk_in, comp_in = arrived(k, 0)
        risk = BASE[k] + (risk_in + CEN[...] * comp_in)
        inv = jnp.where(COD[...] == 1, 1.0 / risk, 0.0)
        heavy = inv * CEN[...]
        TS[k, 1, 0] = fold(heavy)
        TS[k, 1, 1] = fold(inv)
        exchange(k, 1)
        upto, upto_rows = lane_scan(inv, "le")
        later, later_rows = lane_scan(heavy, "gt")
        lanes = LST[...]
        BASE[k] = (pick(upto, lanes) + row_scan(upto_rows, "gt")) + IC2[...] * (
            pick(later, lanes) + row_scan(later_rows, "lt")
        )

    def scan_c(k):
        later_in, early_in = arrived(k, 1)
        event = jnp.where(COD[...] == 1, 1.0, 0.0)
        W5[x, z, k] = event - EX[k] * (BASE[k] + (early_in + IC2[...] * later_in))

    def ag_first(h, k, part):
        start = part * QUART
        rows = pl.ds(h * HALF + start, QUART)
        mine = W5.at[x, z, k, rows, :]
        for at in ring(1 - h):
            send(("a1", h, k, part), mine, mine, device(1 - h, at))

    def ag_second(h, k, part):
        received("a1", h, k, part)
        left, right, opposite = ring(h)
        mine = quarter(W5, h, pos[h], k, part * QUART, QUART)
        for at in (left, right):
            send(("a2", h, k, part), mine, mine, device(h, at))

    def ag_third(h, k, part):
        left, right, opposite = ring(h)
        received("a2", h, k, part)
        for came, to, start in ((left, right, 0), (right, left, QUART // 2)):
            piece = quarter(W5, h, came, k, part * QUART + start, QUART // 2)
            send(("a3", h, k, part), piece, piece, device(h, to))

    def ag_end(h, k, part):
        received("a3", h, k, part)

    def score(k, part, total):
        def body(h, total):
            start = pl.multiple_of((2 * h + part) * CHUNK, CHUNK)
            parts = []
            for j in range(QUART):
                block = (2 * h + part) * QUART + j
                rows = [
                    W[pl.ds((g * 16 + k) * BLOCKS + block, 8, stride=2 * BLOCKS), :]
                    for g in range(2)
                ]
                parts.append(jnp.concatenate(rows, axis=0).astype(BF16))
            return total + dot(jnp.concatenate(parts, axis=1), D[pl.ds(start, CHUNK), :])

        return lax.fori_loop(0, 2, body, total)

    def score_out(k, total):
        SP[k] = total
        for d in range(1, SUBJ):
            send(("s", k), SP.at[k], SR.at[k, s], ((s + d) % SUBJ, cov))
        SR[k, s] = total

    both = (0, 1)
    for i, (chunk, h, part) in enumerate(((0, 0, 0), (2, 1, 0), (1, 0, 1), (3, 1, 1))):
        chunks[chunk].wait()
        predict(chunk)
        if i == 0:
            pl.semaphore_wait(barrier, len(peers))
        rs_far(h, 0, part)
        rs_near(h, 0, part)
    for h in both:
        rs_far(h, 1, 0)
        rs_far(h, 1, 1)
    for h in both:
        rs_on(h, 0)
    for h in both:
        rs_near(h, 1, 0)
        rs_near(h, 1, 1)
    prepare()
    for h in both:
        rs_on(h, 1)
    for k in both:
        for h in both:
            rs_second(h, k)
    for h in both:
        rs_end(h, 0)
    scan_a(0)
    for h in both:
        rs_end(h, 1)
    scan_a(1)
    for k in both:
        scan_b(k)
    for k in both:
        scan_c(k)
        for part in both:
            for h in both:
                ag_first(h, k, part)
    for step in (ag_second, ag_third):
        for k in both:
            for part in both:
                for h in both:
                    step(h, k, part)
    for k in both:
        total = jnp.zeros((PATHS // 2, COLS), F32)
        for part in both:
            for h in both:
                ag_end(h, k, part)
            total = score(k, part, total)
        score_out(k, total)
    outs = []
    for c in range(4):
        part = pl.ds(c * CHUNK, CHUNK)

        def convert(block, carry):
            lanes = pl.ds(pl.multiple_of(block * LANES, LANES), LANES)
            for g in range(4):
                OUTV[g * 8 : g * 8 + 8, lanes] = W[
                    pl.ds(g * 8 * BLOCKS + block, 8, stride=BLOCKS), :
                ]
            return carry

        lax.fori_loop(c * QUART, (c + 1) * QUART, convert, 0, unroll=8)
        copy = pltpu.make_async_copy(OUTV.at[:, part], weights_out.at[:, part], out_sem.at[c])
        copy.start()
        outs.append(copy)
    eye = (
        lax.broadcasted_iota(jnp.int32, (PATHS, PATHS), 0)
        == lax.broadcasted_iota(jnp.int32, (PATHS, PATHS), 1)
    )
    limit = jnp.sum(
        jnp.where(eye, jnp.broadcast_to(PEN[...], (PATHS, PATHS)), 0.0), axis=1, keepdims=True
    )
    wide = C[...].astype(F32)
    for k in both:
        received("s", k)
        total = SR[k, 0]
        for i in range(1, SUBJ):
            total = total + SR[k, i]
        for c in range(2):
            SUM[c, pl.ds(k, PATHS // 2, stride=2), :] = total[:, c * LANES : (c + 1) * LANES]
    scale = 0.1 / jnp.sqrt(F32(SUBJ * ROWS))
    for c in range(2):
        cols = slice(c * LANES, (c + 1) * LANES)
        shifted = wide[:, cols] + scale * SUM[c]
        sign = jnp.where(shifted > 0, 1.0, jnp.where(shifted < 0, -1.0, 0.0))
        new_out[:, cols] = sign * jnp.maximum(jnp.abs(shifted) - limit, 0.0)
    for copy in outs:
        copy.wait()
    left_rows = sent_rows[0]
    span = D.at[pl.ds(0, left_rows), :]
    pltpu.make_async_copy(span, span, send_sem.at[0]).wait()


def hand_over(new, weights, new_out, weights_out, N, V, in_sem, out_sem):
    parts = [(new, N, new_out)]
    for c in range(4):
        part = pl.ds(c * CHUNK, CHUNK)
        parts.append((weights.at[:, part], V.at[:, part], weights_out.at[:, part]))
    ins = [pltpu.make_async_copy(a, b, in_sem.at[i]) for i, (a, b, c) in enumerate(parts)]
    outs = [pltpu.make_async_copy(b, c, out_sem.at[i]) for i, (a, b, c) in enumerate(parts)]
    for copy in ins:
        copy.start()
    for come, go in zip(ins, outs):
        come.wait()
        go.start()
    for go in outs:
        go.wait()


def local(design, coefs, penalty, censor, codes, tie_first, tie_last):
    square = (BLOCKS, LANES)
    vmem = pltpu.VMEM
    dma = pltpu.SemaphoreType.DMA
    new, weights = pl.pallas_call(
        kernel,
        out_shape=(
            jax.ShapeDtypeStruct((PATHS, COLS), F32),
            jax.ShapeDtypeStruct((PATHS, ROWS), F32),
        ),
        in_specs=[pl.BlockSpec(memory_space=pltpu.HBM)] * 7,
        out_specs=(pl.BlockSpec(memory_space=pltpu.VMEM), pl.BlockSpec(memory_space=pltpu.HBM)),
        scratch_shapes=[
            vmem((ROWS, COLS), BF16),
            vmem((PATHS, COLS), BF16),
            vmem((1, PATHS), F32),
            vmem(square, F32),
            vmem(square, jnp.int32),
            vmem(square, jnp.int32),
            vmem(square, jnp.int32),
            vmem(square, F32),
            vmem((PATHS * BLOCKS, LANES), F32),
            vmem((2, NBATCH, 2, RING, QUART, LANES), F32),
            vmem((2, NBATCH, 2, RING, HALF, LANES), F32),
            vmem((2, NBATCH, RING, HALF, LANES), F32),
            vmem((2, NBATCH, 3, HALF, LANES), F32),
            vmem((NBATCH, BLOCKS, LANES), F32),
            vmem((NBATCH, BLOCKS, LANES), F32),
            vmem((NBATCH, BLOCKS, LANES), F32),
            vmem((NBATCH, 2, 2, 8, LANES), F32),
            vmem((NBATCH, 2, SUBJ, 2, 8, LANES), F32),
            vmem((PATHS * BLOCKS, LANES), F32),
            vmem((NBATCH, PATHS // 2, COLS), F32),
            vmem((NBATCH, SUBJ, PATHS // 2, COLS), F32),
            vmem((2, PATHS, LANES), F32),
            vmem((PATHS, ROWS), F32),
            dma((10,)),
            dma((4,)),
            dma((1,)),
            dma((42,)),
        ],
        compiler_params=pltpu.CompilerParams(
            collective_id=0, has_side_effects=True, vmem_limit_bytes=56 * 2**20
        ),
        cost_estimate=pl.CostEstimate(
            flops=4 * PATHS * ROWS * COLS,
            bytes_accessed=2 * ROWS * COLS + 4 * PATHS * ROWS,
            transcendentals=2 * ROWS,
        ),
    )(
        design,
        coefs.T,
        penalty.reshape(1, PATHS),
        censor.reshape(square),
        codes.reshape(square),
        tie_first.reshape(square),
        tie_last.reshape(square),
    )
    new, weights = pl.pallas_call(
        hand_over,
        out_shape=(
            jax.ShapeDtypeStruct((PATHS, COLS), F32),
            jax.ShapeDtypeStruct((PATHS, ROWS), F32),
        ),
        in_specs=[pl.BlockSpec(memory_space=pltpu.HBM)] * 2,
        out_specs=(pl.BlockSpec(memory_space=pltpu.HBM), pl.BlockSpec(memory_space=pltpu.HBM)),
        scratch_shapes=[
            vmem((PATHS, COLS), F32),
            vmem((PATHS, ROWS), F32),
            dma((5,)),
            dma((5,)),
        ],
        compiler_params=pltpu.CompilerParams(vmem_limit_bytes=60 * 2**20),
    )(new, weights)
    return new.T, weights


def solution(mesh):
    in_specs = (P("subj", "cov"), P("cov", None), P(), P("subj"), P("subj"), P("subj"), P("subj"))
    out_specs = (P("cov", None), P(None, "subj"))
    return jax.shard_map(local, mesh=mesh, in_specs=in_specs, out_specs=out_specs, check_vma=False)
```

```python
import functools

import jax
import jax.numpy as jnp
from jax import lax
from jax.experimental import pallas as pl
from jax.experimental.pallas import tpu as pltpu
from jax.sharding import PartitionSpec as P

MESH = pl.DeviceIdType.MESH
F32 = jnp.float32
BF16 = jnp.bfloat16
LANES = 128
SUBJ = 8
RING = 4
PATHS = 32
ROWS = 16384
COLS = 256
BLOCKS = ROWS // LANES
HALF = BLOCKS // 2
QUART = BLOCKS // 4
EIGHTH = BLOCKS // 8
CHUNK = ROWS // 4
NBATCH = 2
CHUNKS = ((0, 0, 16), (1, 0, 16), (0, 16, 16), (1, 16, 16), (0, 32, 16), (1, 32, 16), (0, 48, 16), (1, 48, 16))
FAR_FIRST = (4, 3, 5, 2, 6, 1, 7)


def split3(x):
    high = x.astype(BF16)
    rest = x - high.astype(F32)
    mid = rest.astype(BF16)
    low = (rest - mid.astype(F32)).astype(BF16)
    return high, mid, low


def dot(a, b):
    return jnp.dot(a, b, preferred_element_type=F32)


def table(kind, wide):
    shape = (LANES, 2 * LANES if wide else LANES)
    row = lax.broadcasted_iota(jnp.int32, shape, 0)
    col = lax.broadcasted_iota(jnp.int32, shape, 1)
    keep = {"ge": row >= col, "lt": row < col, "le": row <= col, "gt": row > col}[kind]
    if wide:
        keep = keep | (col >= LANES)
    return jnp.where(keep, 1.0, 0.0).astype(BF16)


def lane_scan(x, kind):
    wide = table(kind, True)
    high, mid, low = split3(x)
    both = dot(high, wide) + (dot(mid, wide) + dot(low, wide))
    return both[:, :LANES], both[:, LANES:]


def row_scan(totals, kind):
    side = table(kind, False)
    high, mid, low = split3(totals)
    return dot(side, high) + (dot(side, mid) + dot(side, low))


def pick(values, lanes):
    return jnp.take_along_axis(values, lanes, axis=1)


def fold(x):
    return x.reshape(BLOCKS // 8, 8, LANES).sum(axis=0)


def kernel(
    design, coefs, penalty, censor, codes, first, last,
    new_out, weights_out,
    D, C, PEN, CEN, COD, FST, LST, IC2, E, R1, R2, S, R4, ETA, EX, BASE, TS, TR, W, SP, SR, SUM, OUTV,
    load_sem, out_sem, send_sem, recv_sem,
):
    s = lax.axis_index("subj")
    cov = lax.axis_index("cov")
    x = cov // RING
    z = cov % RING
    pos = (x, z)

    E5 = E.reshape(RING, RING, 2, BLOCKS, LANES)
    W5 = W.reshape(RING, RING, 2, BLOCKS, LANES)

    def device(axis, at):
        return (s, at * RING + z) if axis == 0 else (s, x * RING + at)

    def ring(axis):
        me = pos[axis]
        return (me + 3) % RING, (me + 1) % RING, (me + 2) % RING

    sent_rows = [0]
    groups = {}

    def rows_of(ref):
        size = 1
        for n in ref.shape[:-1]:
            size *= n
        return size * ref.shape[-1] // LANES

    def send(group, src, dst, to):
        at, rows = groups.get(group, (len(groups), 0))
        groups[group] = (at, rows + rows_of(src))
        sent_rows[0] += rows_of(src)
        pltpu.make_async_remote_copy(
            src_ref=src, dst_ref=dst, send_sem=send_sem.at[0], recv_sem=recv_sem.at[at],
            device_id=to, device_id_type=MESH,
        ).start()

    def wait_rows(sem, rows):
        span = W.at[pl.ds(0, rows), :]
        pltpu.make_async_copy(span, span, sem).wait()

    def received(*group):
        at, rows = groups[group]
        wait_rows(recv_sem.at[at], rows)

    barrier = pltpu.get_barrier_semaphore()
    peers = [device(axis, at) for axis in (0, 1) for at in ring(axis)]
    peers += [((s + d) % SUBJ, cov) for d in range(1, SUBJ)]
    for peer in peers:
        pl.semaphore_signal(barrier, inc=1, device_id=peer, device_id_type=MESH)

    chunks = []
    for i, (h, first_block, blocks) in enumerate(CHUNKS):
        part = pl.ds((h * HALF + first_block) * LANES, blocks * LANES)
        chunks.append(pltpu.make_async_copy(design.at[part], D.at[part], load_sem.at[i]))
    small = []
    for i, (src, dst) in enumerate(
        [(coefs, C), (penalty, PEN), (censor, CEN), (codes, COD), (first, FST), (last, LST)]
    ):
        small.append(pltpu.make_async_copy(src, dst, load_sem.at[len(CHUNKS) + i]))
    small[0].start()
    for copy in chunks:
        copy.start()
    for copy in small[1:]:
        copy.start()

    small[0].wait()
    nt = (((1,), (1,)), ((), ()))
    lhs = C[...]

    def predict(h, first_block, blocks):
        start = (h * HALF + first_block) * LANES
        part = lax.dot_general(
            lhs, D[start : start + blocks * LANES, :], nt, preferred_element_type=F32
        )
        for j in range(blocks):
            block = h * HALF + first_block + j
            for g in range(4):
                E[pl.ds(g * 8 * BLOCKS + block, 8, stride=BLOCKS), :] = part[
                    g * 8 : g * 8 + 8, j * LANES : (j + 1) * LANES
                ]

    def quarter(ref, half, at, k, start, size):
        rows = pl.ds(half * HALF + start, size)
        return ref.at[at, :, k, rows, :] if half == 0 else ref.at[:, at, k, rows, :]

    def rs_far(h, k, part, d):
        left, right, opposite = ring(h)
        start = part * QUART + d * EIGHTH
        send(
            ("m1", h, k, part),
            quarter(E5, h, opposite, k, start, EIGHTH),
            R1.at[h, k, part, d],
            device(h, left if d else right),
        )

    def rs_near(h, k, part, d):
        left, right, opposite = ring(h)
        start = part * QUART + d * EIGHTH
        to = right if d else left
        send(
            ("m2", h, k, part),
            quarter(E5, h, to, k, start, EIGHTH),
            R2.at[h, k, 1 - d, :, pl.ds(start, EIGHTH), :],
            device(h, to),
        )

    def rs_on(h, k, part):
        left, right, opposite = ring(h)
        received("m1", h, k, part)
        for d, to in ((0, right), (1, left)):
            start = part * QUART + d * EIGHTH
            mine = quarter(E5, h, to, k, start, EIGHTH)
            mine[...] = mine[...] + R1[h, k, part, d]
            send(
                ("m2", h, k, part),
                mine,
                R2.at[h, k, d, :, pl.ds(start, EIGHTH), :],
                device(h, to),
            )

    def rs_second(h, k, part):
        received("m2", h, k, part)
        rows = pl.ds(part * QUART, QUART)
        S[h, k, :, rows, :] = (
            quarter(E5, h, pos[h], k, part * QUART, QUART)[...]
            + R2[h, k, 0, :, rows, :]
            + R2[h, k, 1, :, rows, :]
        )
        for slot, at in reversed(list(enumerate(ring(1 - h)))):
            send(("n", h, k), S.at[h, k, at, rows, :], R4.at[h, k, slot, rows, :], device(1 - h, at))

    def rs_end(h, k):
        received("n", h, k)
        ETA[k, pl.ds(h * HALF, HALF), :] = S[h, k, pos[1 - h]] + (
            R4[h, k, 0] + R4[h, k, 1] + R4[h, k, 2]
        )

    def exchange(k, e):
        for d in FAR_FIRST:
            send(("t", k, e), TS.at[k, e], TR.at[k, e, d], ((s + d) % SUBJ, cov))

    def arrived(k, e):
        received("t", k, e)
        after = jnp.zeros((8, LANES), F32)
        before = jnp.zeros((8, LANES), F32)
        for d in range(1, SUBJ):
            after = after + jnp.where(d > s, TR[k, e, d, 0], 0.0)
            before = before + jnp.where(d <= s, TR[k, e, d, 1], 0.0)
        return jnp.sum(after, keepdims=True), jnp.sum(before, keepdims=True)

    def prepare():
        for copy in small[1:]:
            copy.wait()
        FST[...] = FST[...] & (LANES - 1)
        LST[...] = LST[...] & (LANES - 1)
        IC2[...] = jnp.where(COD[...] == 2, 1.0 / CEN[...], 0.0)

    def scan_a(k):
        expo = jnp.exp(ETA[k])
        comp = expo * IC2[...]
        EX[k] = expo
        TS[k, 0, 0] = fold(expo)
        TS[k, 0, 1] = fold(comp)
        exchange(k, 0)
        risk, risk_rows = lane_scan(expo, "ge")
        before, before_rows = lane_scan(comp, "lt")
        lanes = FST[...]
        BASE[k] = (pick(risk, lanes) + row_scan(risk_rows, "lt")) + CEN[...] * (
            pick(before, lanes) + row_scan(before_rows, "gt")
        )

    def scan_b(k):
        risk_in, comp_in = arrived(k, 0)
        risk = BASE[k] + (risk_in + CEN[...] * comp_in)
        inv = jnp.where(COD[...] == 1, 1.0 / risk, 0.0)
        heavy = inv * CEN[...]
        TS[k, 1, 0] = fold(heavy)
        TS[k, 1, 1] = fold(inv)
        exchange(k, 1)
        upto, upto_rows = lane_scan(inv, "le")
        later, later_rows = lane_scan(heavy, "gt")
        lanes = LST[...]
        BASE[k] = (pick(upto, lanes) + row_scan(upto_rows, "gt")) + IC2[...] * (
            pick(later, lanes) + row_scan(later_rows, "lt")
        )

    def scan_c(k):
        later_in, early_in = arrived(k, 1)
        event = jnp.where(COD[...] == 1, 1.0, 0.0)
        W5[x, z, k] = event - EX[k] * (BASE[k] + (early_in + IC2[...] * later_in))

    def ag_first(h, k, part):
        start = part * QUART
        rows = pl.ds(h * HALF + start, QUART)
        mine = W5.at[x, z, k, rows, :]
        for at in reversed(ring(1 - h)):
            send(("a1", h, k, part), mine, mine, device(1 - h, at))

    def ag_second(h, k, part):
        received("a1", h, k, part)
        left, right, opposite = ring(h)
        mine = quarter(W5, h, pos[h], k, part * QUART, QUART)
        for at in (left, right):
            send(("a2", h, k, part), mine, mine, device(h, at))

    def ag_third(h, k, part):
        left, right, opposite = ring(h)
        received("a2", h, k, part)
        for came, to, start in ((left, right, 0), (right, left, QUART // 2)):
            piece = quarter(W5, h, came, k, part * QUART + start, QUART // 2)
            send(("a3", h, k, part), piece, piece, device(h, to))

    def ag_end(h, k, part):
        received("a3", h, k, part)

    def score(k, part, total):
        def body(h, total):
            start = pl.multiple_of((2 * h + part) * CHUNK, CHUNK)
            parts = []
            for j in range(QUART):
                block = (2 * h + part) * QUART + j
                rows = [
                    W[pl.ds((g * 16 + k) * BLOCKS + block, 8, stride=2 * BLOCKS), :]
                    for g in range(2)
                ]
                parts.append(jnp.concatenate(rows, axis=0).astype(BF16))
            return total + dot(jnp.concatenate(parts, axis=1), D[pl.ds(start, CHUNK), :])

        return lax.fori_loop(0, 2, body, total)

    def score_out(k, total):
        SP[k] = total
        for d in FAR_FIRST:
            send(("s", k), SP.at[k], SR.at[k, s], ((s + d) % SUBJ, cov))
        SR[k, s] = total

    both = (0, 1)
    both = (0, 1)
    for i, (h, first_block, blocks) in enumerate(CHUNKS):
        chunks[i].wait()
        predict(h, first_block, blocks)
        if i == 0:
            pl.semaphore_wait(barrier, len(peers))
        for at in range(first_block // EIGHTH, (first_block + blocks) // EIGHTH):
            part, d = at // 2, at % 2
            rs_far(h, 0, part, d)
            rs_near(h, 0, part, d)
            rs_far(h, 1, part, d)
    for h in both:
        rs_on(h, 0, 0)
    for h in both:
        for d in both:
            rs_near(h, 1, 0, d)
    for h in both:
        rs_on(h, 0, 1)
    for h in both:
        for d in both:
            rs_near(h, 1, 1, d)
    prepare()
    for h in both:
        rs_on(h, 1, 0)
    for h in both:
        rs_second(h, 0, 0)
    for h in both:
        rs_on(h, 1, 1)
    for h in both:
        rs_second(h, 0, 1)
    for h in both:
        rs_second(h, 1, 0)
    for h in both:
        rs_second(h, 1, 1)
    for h in both:
        rs_end(h, 0)
    scan_a(0)
    for h in both:
        rs_end(h, 1)
    scan_a(1)
    for k in both:
        scan_b(k)
    for k in both:
        scan_c(k)
        for part in both:
            for h in both:
                ag_first(h, k, part)
    for step in (ag_second, ag_third):
        for k in both:
            for part in both:
                for h in both:
                    step(h, k, part)
    for k in both:
        total = jnp.zeros((PATHS // 2, COLS), F32)
        for part in both:
            for h in both:
                ag_end(h, k, part)
            total = score(k, part, total)
        score_out(k, total)
    outs = []
    for c in range(4):
        part = pl.ds(c * CHUNK, CHUNK)

        def convert(block, carry):
            lanes = pl.ds(pl.multiple_of(block * LANES, LANES), LANES)
            for g in range(4):
                OUTV[g * 8 : g * 8 + 8, lanes] = W[
                    pl.ds(g * 8 * BLOCKS + block, 8, stride=BLOCKS), :
                ]
            return carry

        lax.fori_loop(c * QUART, (c + 1) * QUART, convert, 0, unroll=8)
        copy = pltpu.make_async_copy(OUTV.at[:, part], weights_out.at[:, part], out_sem.at[c])
        copy.start()
        outs.append(copy)
    eye = (
        lax.broadcasted_iota(jnp.int32, (PATHS, PATHS), 0)
        == lax.broadcasted_iota(jnp.int32, (PATHS, PATHS), 1)
    )
    limit = jnp.sum(
        jnp.where(eye, jnp.broadcast_to(PEN[...], (PATHS, PATHS)), 0.0), axis=1, keepdims=True
    )
    wide = C[...].astype(F32)
    for k in both:
        received("s", k)
        total = SR[k, 0]
        for i in range(1, SUBJ):
            total = total + SR[k, i]
        for c in range(2):
            SUM[c, pl.ds(k, PATHS // 2, stride=2), :] = total[:, c * LANES : (c + 1) * LANES]
    scale = 0.1 / jnp.sqrt(F32(SUBJ * ROWS))
    for c in range(2):
        cols = slice(c * LANES, (c + 1) * LANES)
        shifted = wide[:, cols] + scale * SUM[c]
        sign = jnp.where(shifted > 0, 1.0, jnp.where(shifted < 0, -1.0, 0.0))
        new_out[:, cols] = sign * jnp.maximum(jnp.abs(shifted) - limit, 0.0)
    for copy in outs:
        copy.wait()
    left_rows = sent_rows[0]
    span = D.at[pl.ds(0, left_rows), :]
    pltpu.make_async_copy(span, span, send_sem.at[0]).wait()


def hand_over(new, weights, new_out, weights_out, N, V, in_sem, out_sem):
    parts = [(new, N, new_out)]
    for c in range(4):
        part = pl.ds(c * CHUNK, CHUNK)
        parts.append((weights.at[:, part], V.at[:, part], weights_out.at[:, part]))
    ins = [pltpu.make_async_copy(a, b, in_sem.at[i]) for i, (a, b, c) in enumerate(parts)]
    outs = [pltpu.make_async_copy(b, c, out_sem.at[i]) for i, (a, b, c) in enumerate(parts)]
    for copy in ins:
        copy.start()
    for come, go in zip(ins, outs):
        come.wait()
        go.start()
    for go in outs:
        go.wait()


def local(design, coefs, penalty, censor, codes, tie_first, tie_last):
    square = (BLOCKS, LANES)
    vmem = pltpu.VMEM
    dma = pltpu.SemaphoreType.DMA
    new, weights = pl.pallas_call(
        kernel,
        out_shape=(
            jax.ShapeDtypeStruct((PATHS, COLS), F32),
            jax.ShapeDtypeStruct((PATHS, ROWS), F32),
        ),
        in_specs=[pl.BlockSpec(memory_space=pltpu.HBM)] * 7,
        out_specs=(pl.BlockSpec(memory_space=pltpu.VMEM), pl.BlockSpec(memory_space=pltpu.HBM)),
        scratch_shapes=[
            vmem((ROWS, COLS), BF16),
            vmem((PATHS, COLS), BF16),
            vmem((1, PATHS), F32),
            vmem(square, F32),
            vmem(square, jnp.int32),
            vmem(square, jnp.int32),
            vmem(square, jnp.int32),
            vmem(square, F32),
            vmem((PATHS * BLOCKS, LANES), F32),
            vmem((2, NBATCH, 2, 2, RING, EIGHTH, LANES), F32),
            vmem((2, NBATCH, 2, RING, HALF, LANES), F32),
            vmem((2, NBATCH, RING, HALF, LANES), F32),
            vmem((2, NBATCH, 3, HALF, LANES), F32),
            vmem((NBATCH, BLOCKS, LANES), F32),
            vmem((NBATCH, BLOCKS, LANES), F32),
            vmem((NBATCH, BLOCKS, LANES), F32),
            vmem((NBATCH, 2, 2, 8, LANES), F32),
            vmem((NBATCH, 2, SUBJ, 2, 8, LANES), F32),
            vmem((PATHS * BLOCKS, LANES), F32),
            vmem((NBATCH, PATHS // 2, COLS), F32),
            vmem((NBATCH, SUBJ, PATHS // 2, COLS), F32),
            vmem((2, PATHS, LANES), F32),
            vmem((PATHS, ROWS), F32),
            dma((len(CHUNKS) + 6,)),
            dma((4,)),
            dma((1,)),
            dma((50,)),
        ],
        compiler_params=pltpu.CompilerParams(
            collective_id=0, has_side_effects=True, vmem_limit_bytes=56 * 2**20
        ),
        cost_estimate=pl.CostEstimate(
            flops=4 * PATHS * ROWS * COLS,
            bytes_accessed=2 * ROWS * COLS + 4 * PATHS * ROWS,
            transcendentals=2 * ROWS,
        ),
    )(
        design,
        coefs.T,
        penalty.reshape(1, PATHS),
        censor.reshape(square),
        codes.reshape(square),
        tie_first.reshape(square),
        tie_last.reshape(square),
    )
    new, weights = pl.pallas_call(
        hand_over,
        out_shape=(
            jax.ShapeDtypeStruct((PATHS, COLS), F32),
            jax.ShapeDtypeStruct((PATHS, ROWS), F32),
        ),
        in_specs=[pl.BlockSpec(memory_space=pltpu.HBM)] * 2,
        out_specs=(pl.BlockSpec(memory_space=pltpu.HBM), pl.BlockSpec(memory_space=pltpu.HBM)),
        scratch_shapes=[
            vmem((PATHS, COLS), F32),
            vmem((PATHS, ROWS), F32),
            dma((5,)),
            dma((5,)),
        ],
        compiler_params=pltpu.CompilerParams(vmem_limit_bytes=60 * 2**20),
    )(new, weights)
    return new.T, weights


def solution(mesh):
    in_specs = (P("subj", "cov"), P("cov", None), P(), P("subj"), P("subj"), P("subj"), P("subj"))
    out_specs = (P("cov", None), P(None, "subj"))
    return jax.shard_map(local, mesh=mesh, in_specs=in_specs, out_specs=out_specs, check_vma=False)
```

```python
import functools

import jax
import jax.numpy as jnp
from jax import lax
from jax.experimental import pallas as pl
from jax.experimental.pallas import tpu as pltpu
from jax.sharding import PartitionSpec as P

MESH = pl.DeviceIdType.MESH
F32 = jnp.float32
BF16 = jnp.bfloat16
LANES = 128
SUBJ = 8
RING = 4
PATHS = 32
ROWS = 16384
COLS = 256
BLOCKS = ROWS // LANES
HALF = BLOCKS // 2
QUART = BLOCKS // 4
EIGHTH = BLOCKS // 8
CHUNK = ROWS // 4
NBATCH = 2
CHUNKS = ((0, 0, 16), (1, 0, 16), (0, 16, 16), (1, 16, 16), (0, 32, 16), (1, 32, 16), (0, 48, 16), (1, 48, 16))
FAR_FIRST = (4, 3, 5, 2, 6, 1, 7)


def split3(x):
    high = x.astype(BF16)
    rest = x - high.astype(F32)
    mid = rest.astype(BF16)
    low = (rest - mid.astype(F32)).astype(BF16)
    return high, mid, low


def dot(a, b):
    return jnp.dot(a, b, preferred_element_type=F32)


def table(kind, wide):
    shape = (LANES, 2 * LANES if wide else LANES)
    row = lax.broadcasted_iota(jnp.int32, shape, 0)
    col = lax.broadcasted_iota(jnp.int32, shape, 1)
    keep = {"ge": row >= col, "lt": row < col, "le": row <= col, "gt": row > col}[kind]
    if wide:
        keep = keep | (col >= LANES)
    return jnp.where(keep, 1.0, 0.0).astype(BF16)


def lane_scan(x, kind):
    wide = table(kind, True)
    high, mid, low = split3(x)
    both = dot(high, wide) + (dot(mid, wide) + dot(low, wide))
    return both[:, :LANES], both[:, LANES:]


def row_scan(totals, kind):
    side = table(kind, False)
    high, mid, low = split3(totals)
    return dot(side, high) + (dot(side, mid) + dot(side, low))


def pick(values, lanes):
    return jnp.take_along_axis(values, lanes, axis=1)


def fold(x):
    return x.reshape(BLOCKS // 8, 8, LANES).sum(axis=0)


def kernel(
    design, coefs, penalty, censor, codes, first, last,
    new_out, weights_out,
    D, C, PEN, CEN, COD, FST, LST, IC2, E, R1, R2, S, R4, ETA, EX, BASE, TS, TR, W, SP, SR, SUM,
    load_sem, send_sem, recv_sem,
):
    s = lax.axis_index("subj")
    cov = lax.axis_index("cov")
    x = cov // RING
    z = cov % RING
    pos = (x, z)

    E5 = E.reshape(RING, RING, 2, BLOCKS, LANES)
    W5 = W.reshape(RING, RING, 2, BLOCKS, LANES)

    def device(axis, at):
        return (s, at * RING + z) if axis == 0 else (s, x * RING + at)

    def ring(axis):
        me = pos[axis]
        return (me + 3) % RING, (me + 1) % RING, (me + 2) % RING

    sent_rows = [0]
    groups = {}

    def rows_of(ref):
        size = 1
        for n in ref.shape[:-1]:
            size *= n
        return size * ref.shape[-1] // LANES

    def send(group, src, dst, to):
        at, rows = groups.get(group, (len(groups), 0))
        groups[group] = (at, rows + rows_of(src))
        sent_rows[0] += rows_of(src)
        pltpu.make_async_remote_copy(
            src_ref=src, dst_ref=dst, send_sem=send_sem.at[0], recv_sem=recv_sem.at[at],
            device_id=to, device_id_type=MESH,
        ).start()

    def wait_rows(sem, rows):
        span = W.at[pl.ds(0, rows), :]
        pltpu.make_async_copy(span, span, sem).wait()

    def received(*group):
        at, rows = groups[group]
        wait_rows(recv_sem.at[at], rows)

    barrier = pltpu.get_barrier_semaphore()
    peers = [device(axis, at) for axis in (0, 1) for at in ring(axis)]
    peers += [((s + d) % SUBJ, cov) for d in range(1, SUBJ)]
    for peer in peers:
        pl.semaphore_signal(barrier, inc=1, device_id=peer, device_id_type=MESH)

    chunks = []
    for i, (h, first_block, blocks) in enumerate(CHUNKS):
        part = pl.ds((h * HALF + first_block) * LANES, blocks * LANES)
        chunks.append(pltpu.make_async_copy(design.at[part], D.at[part], load_sem.at[i]))
    small = []
    for i, (src, dst) in enumerate(
        [(coefs, C), (penalty, PEN), (censor, CEN), (codes, COD), (first, FST), (last, LST)]
    ):
        small.append(pltpu.make_async_copy(src, dst, load_sem.at[len(CHUNKS) + i]))
    small[0].start()
    for copy in chunks:
        copy.start()
    for copy in small[1:]:
        copy.start()

    small[0].wait()
    nt = (((1,), (1,)), ((), ()))
    lhs = C[...]

    def predict(h, first_block, blocks):
        start = (h * HALF + first_block) * LANES
        part = lax.dot_general(
            lhs, D[start : start + blocks * LANES, :], nt, preferred_element_type=F32
        )
        for j in range(blocks):
            block = h * HALF + first_block + j
            for g in range(4):
                E[pl.ds(g * 8 * BLOCKS + block, 8, stride=BLOCKS), :] = part[
                    g * 8 : g * 8 + 8, j * LANES : (j + 1) * LANES
                ]

    def quarter(ref, half, at, k, start, size):
        rows = pl.ds(half * HALF + start, size)
        return ref.at[at, :, k, rows, :] if half == 0 else ref.at[:, at, k, rows, :]

    def rs_far(h, k, part, d):
        left, right, opposite = ring(h)
        start = part * QUART + d * EIGHTH
        send(
            ("m1", h, k, part),
            quarter(E5, h, opposite, k, start, EIGHTH),
            R1.at[h, k, part, d],
            device(h, left if d else right),
        )

    def rs_near(h, k, part, d):
        left, right, opposite = ring(h)
        start = part * QUART + d * EIGHTH
        to = right if d else left
        send(
            ("m2", h, k, part),
            quarter(E5, h, to, k, start, EIGHTH),
            R2.at[h, k, 1 - d, :, pl.ds(start, EIGHTH), :],
            device(h, to),
        )

    def rs_on(h, k, part):
        left, right, opposite = ring(h)
        received("m1", h, k, part)
        for d, to in ((0, right), (1, left)):
            start = part * QUART + d * EIGHTH
            mine = quarter(E5, h, to, k, start, EIGHTH)
            mine[...] = mine[...] + R1[h, k, part, d]
            send(
                ("m2", h, k, part),
                mine,
                R2.at[h, k, d, :, pl.ds(start, EIGHTH), :],
                device(h, to),
            )

    def rs_second(h, k, part):
        received("m2", h, k, part)
        rows = pl.ds(part * QUART, QUART)
        S[h, k, :, rows, :] = (
            quarter(E5, h, pos[h], k, part * QUART, QUART)[...]
            + R2[h, k, 0, :, rows, :]
            + R2[h, k, 1, :, rows, :]
        )
        for slot, at in reversed(list(enumerate(ring(1 - h)))):
            send(("n", h, k), S.at[h, k, at, rows, :], R4.at[h, k, slot, rows, :], device(1 - h, at))

    def rs_end(h, k):
        received("n", h, k)
        ETA[k, pl.ds(h * HALF, HALF), :] = S[h, k, pos[1 - h]] + (
            R4[h, k, 0] + R4[h, k, 1] + R4[h, k, 2]
        )

    def exchange(k, e):
        for d in FAR_FIRST:
            send(("t", k, e), TS.at[k, e], TR.at[k, e, d], ((s + d) % SUBJ, cov))

    def arrived(k, e):
        received("t", k, e)
        after = jnp.zeros((8, LANES), F32)
        before = jnp.zeros((8, LANES), F32)
        for d in range(1, SUBJ):
            after = after + jnp.where(d > s, TR[k, e, d, 0], 0.0)
            before = before + jnp.where(d <= s, TR[k, e, d, 1], 0.0)
        return jnp.sum(after, keepdims=True), jnp.sum(before, keepdims=True)

    def prepare():
        for copy in small[1:]:
            copy.wait()
        FST[...] = FST[...] & (LANES - 1)
        LST[...] = LST[...] & (LANES - 1)
        IC2[...] = jnp.where(COD[...] == 2, 1.0 / CEN[...], 0.0)

    def scan_a(k):
        expo = jnp.exp(ETA[k])
        comp = expo * IC2[...]
        EX[k] = expo
        TS[k, 0, 0] = fold(expo)
        TS[k, 0, 1] = fold(comp)
        exchange(k, 0)
        risk, risk_rows = lane_scan(expo, "ge")
        before, before_rows = lane_scan(comp, "lt")
        lanes = FST[...]
        BASE[k] = (pick(risk, lanes) + row_scan(risk_rows, "lt")) + CEN[...] * (
            pick(before, lanes) + row_scan(before_rows, "gt")
        )

    def scan_b(k):
        risk_in, comp_in = arrived(k, 0)
        risk = BASE[k] + (risk_in + CEN[...] * comp_in)
        inv = jnp.where(COD[...] == 1, 1.0 / risk, 0.0)
        heavy = inv * CEN[...]
        TS[k, 1, 0] = fold(heavy)
        TS[k, 1, 1] = fold(inv)
        exchange(k, 1)
        upto, upto_rows = lane_scan(inv, "le")
        later, later_rows = lane_scan(heavy, "gt")
        lanes = LST[...]
        BASE[k] = (pick(upto, lanes) + row_scan(upto_rows, "gt")) + IC2[...] * (
            pick(later, lanes) + row_scan(later_rows, "lt")
        )

    def scan_c(k):
        later_in, early_in = arrived(k, 1)
        event = jnp.where(COD[...] == 1, 1.0, 0.0)
        W5[x, z, k] = event - EX[k] * (BASE[k] + (early_in + IC2[...] * later_in))

    def ag_first(h, k, part):
        start = part * QUART
        rows = pl.ds(h * HALF + start, QUART)
        mine = W5.at[x, z, k, rows, :]
        for at in reversed(ring(1 - h)):
            send(("a1", h, k, part), mine, mine, device(1 - h, at))

    def ag_second(h, k, part):
        received("a1", h, k, part)
        left, right, opposite = ring(h)
        mine = quarter(W5, h, pos[h], k, part * QUART, QUART)
        for at in (left, right):
            send(("a2", h, k, part), mine, mine, device(h, at))

    def ag_third(h, k, part):
        left, right, opposite = ring(h)
        received("a2", h, k, part)
        for came, to, start in ((left, right, 0), (right, left, QUART // 2)):
            piece = quarter(W5, h, came, k, part * QUART + start, QUART // 2)
            send(("a3", h, k, part), piece, piece, device(h, to))

    def ag_end(h, k, part):
        received("a3", h, k, part)

    def score(k, part, total):
        def body(h, total):
            start = pl.multiple_of((2 * h + part) * CHUNK, CHUNK)
            parts = []
            for j in range(QUART):
                block = (2 * h + part) * QUART + j
                rows = [
                    W[pl.ds((g * 16 + k) * BLOCKS + block, 8, stride=2 * BLOCKS), :]
                    for g in range(2)
                ]
                parts.append(jnp.concatenate(rows, axis=0).astype(BF16))
            return total + dot(jnp.concatenate(parts, axis=1), D[pl.ds(start, CHUNK), :])

        return lax.fori_loop(0, 2, body, total)

    def score_out(k, total):
        SP[k] = total
        for d in FAR_FIRST:
            send(("s", k), SP.at[k], SR.at[k, s], ((s + d) % SUBJ, cov))
        SR[k, s] = total

    both = (0, 1)
    both = (0, 1)
    for i, (h, first_block, blocks) in enumerate(CHUNKS):
        chunks[i].wait()
        predict(h, first_block, blocks)
        if i == 0:
            pl.semaphore_wait(barrier, len(peers))
        for at in range(first_block // EIGHTH, (first_block + blocks) // EIGHTH):
            part, d = at // 2, at % 2
            rs_far(h, 0, part, d)
            rs_near(h, 0, part, d)
            rs_far(h, 1, part, d)
    for h in both:
        rs_on(h, 0, 0)
    for h in both:
        for d in both:
            rs_near(h, 1, 0, d)
    for h in both:
        rs_on(h, 0, 1)
    for h in both:
        for d in both:
            rs_near(h, 1, 1, d)
    prepare()
    for h in both:
        rs_on(h, 1, 0)
    for h in both:
        rs_second(h, 0, 0)
    for h in both:
        rs_on(h, 1, 1)
    for h in both:
        rs_second(h, 0, 1)
    for h in both:
        rs_second(h, 1, 0)
    for h in both:
        rs_second(h, 1, 1)
    for h in both:
        rs_end(h, 0)
    scan_a(0)
    for h in both:
        rs_end(h, 1)
    scan_a(1)
    for k in both:
        scan_b(k)
    for k in both:
        scan_c(k)
        for part in both:
            for h in both:
                ag_first(h, k, part)
    for step in (ag_second, ag_third):
        for k in both:
            for part in both:
                for h in both:
                    step(h, k, part)
    for k in both:
        total = jnp.zeros((PATHS // 2, COLS), F32)
        for part in both:
            for h in both:
                ag_end(h, k, part)
            total = score(k, part, total)
        score_out(k, total)

    def convert(block, carry):
        lanes = pl.ds(pl.multiple_of(block * LANES, LANES), LANES)
        for g in range(4):
            weights_out[g * 8 : g * 8 + 8, lanes] = W[
                pl.ds(g * 8 * BLOCKS + block, 8, stride=BLOCKS), :
            ]
        return carry

    lax.fori_loop(0, BLOCKS, convert, 0, unroll=8)
    eye = (
        lax.broadcasted_iota(jnp.int32, (PATHS, PATHS), 0)
        == lax.broadcasted_iota(jnp.int32, (PATHS, PATHS), 1)
    )
    limit = jnp.sum(
        jnp.where(eye, jnp.broadcast_to(PEN[...], (PATHS, PATHS)), 0.0), axis=1, keepdims=True
    )
    wide = C[...].astype(F32)
    for k in both:
        received("s", k)
        total = SR[k, 0]
        for i in range(1, SUBJ):
            total = total + SR[k, i]
        for c in range(2):
            SUM[c, pl.ds(k, PATHS // 2, stride=2), :] = total[:, c * LANES : (c + 1) * LANES]
    scale = 0.1 / jnp.sqrt(F32(SUBJ * ROWS))
    for c in range(2):
        cols = slice(c * LANES, (c + 1) * LANES)
        shifted = wide[:, cols] + scale * SUM[c]
        sign = jnp.where(shifted > 0, 1.0, jnp.where(shifted < 0, -1.0, 0.0))
        new_out[:, cols] = sign * jnp.maximum(jnp.abs(shifted) - limit, 0.0)
    left_rows = sent_rows[0]
    span = D.at[pl.ds(0, left_rows), :]
    pltpu.make_async_copy(span, span, send_sem.at[0]).wait()


def hand_over(new, weights, new_out, weights_out, sem):
    copies = [pltpu.make_async_copy(new, new_out, sem.at[4])]
    for c in range(4):
        rows = pl.ds(c * 8, 8)
        copies.append(pltpu.make_async_copy(weights.at[rows], weights_out.at[rows], sem.at[c]))
    for copy in copies:
        copy.start()
    for copy in copies:
        copy.wait()


def local(design, coefs, penalty, censor, codes, tie_first, tie_last):
    square = (BLOCKS, LANES)
    vmem = pltpu.VMEM
    dma = pltpu.SemaphoreType.DMA
    new, weights = pl.pallas_call(
        kernel,
        out_shape=(
            jax.ShapeDtypeStruct((PATHS, COLS), F32),
            jax.ShapeDtypeStruct((PATHS, ROWS), F32),
        ),
        in_specs=[pl.BlockSpec(memory_space=pltpu.HBM)] * 7,
        out_specs=(pl.BlockSpec(memory_space=pltpu.VMEM), pl.BlockSpec(memory_space=pltpu.VMEM)),
        scratch_shapes=[
            vmem((ROWS, COLS), BF16),
            vmem((PATHS, COLS), BF16),
            vmem((1, PATHS), F32),
            vmem(square, F32),
            vmem(square, jnp.int32),
            vmem(square, jnp.int32),
            vmem(square, jnp.int32),
            vmem(square, F32),
            vmem((PATHS * BLOCKS, LANES), F32),
            vmem((2, NBATCH, 2, 2, RING, EIGHTH, LANES), F32),
            vmem((2, NBATCH, 2, RING, HALF, LANES), F32),
            vmem((2, NBATCH, RING, HALF, LANES), F32),
            vmem((2, NBATCH, 3, HALF, LANES), F32),
            vmem((NBATCH, BLOCKS, LANES), F32),
            vmem((NBATCH, BLOCKS, LANES), F32),
            vmem((NBATCH, BLOCKS, LANES), F32),
            vmem((NBATCH, 2, 2, 8, LANES), F32),
            vmem((NBATCH, 2, SUBJ, 2, 8, LANES), F32),
            vmem((PATHS * BLOCKS, LANES), F32),
            vmem((NBATCH, PATHS // 2, COLS), F32),
            vmem((NBATCH, SUBJ, PATHS // 2, COLS), F32),
            vmem((2, PATHS, LANES), F32),
            dma((len(CHUNKS) + 6,)),
            dma((1,)),
            dma((50,)),
        ],
        compiler_params=pltpu.CompilerParams(
            collective_id=0, has_side_effects=True, vmem_limit_bytes=48 * 2**20
        ),
        cost_estimate=pl.CostEstimate(
            flops=4 * PATHS * ROWS * COLS,
            bytes_accessed=2 * ROWS * COLS + 4 * PATHS * ROWS,
            transcendentals=2 * ROWS,
        ),
    )(
        *(
            pltpu.with_memory_space_constraint(a, pltpu.HBM)
            for a in (
                design,
                coefs.T,
                penalty.reshape(1, PATHS),
                censor.reshape(square),
                codes.reshape(square),
                tie_first.reshape(square),
                tie_last.reshape(square),
            )
        )
    )
    new, weights = pl.pallas_call(
        hand_over,
        out_shape=(
            jax.ShapeDtypeStruct((PATHS, COLS), F32),
            jax.ShapeDtypeStruct((PATHS, ROWS), F32),
        ),
        in_specs=[pl.BlockSpec(memory_space=pltpu.VMEM)] * 2,
        out_specs=(pl.BlockSpec(memory_space=pltpu.HBM), pl.BlockSpec(memory_space=pltpu.HBM)),
        scratch_shapes=[dma((5,))],
        compiler_params=pltpu.CompilerParams(vmem_limit_bytes=40 * 2**20),
    )(new, weights)
    return new.T, weights


def solution(mesh):
    in_specs = (P("subj", "cov"), P("cov", None), P(), P("subj"), P("subj"), P("subj"), P("subj"))
    out_specs = (P("cov", None), P(None, "subj"))
    return jax.shard_map(local, mesh=mesh, in_specs=in_specs, out_specs=out_specs, check_vma=False)
```

```python
import functools

import jax
import jax.numpy as jnp
from jax import lax
from jax.experimental import pallas as pl
from jax.experimental.pallas import tpu as pltpu
from jax.sharding import PartitionSpec as P

MESH = pl.DeviceIdType.MESH
F32 = jnp.float32
BF16 = jnp.bfloat16
LANES = 128
SUBJ = 8
RING = 4
PATHS = 32
ROWS = 16384
COLS = 256
BLOCKS = ROWS // LANES
HALF = BLOCKS // 2
QUART = BLOCKS // 4
EIGHTH = BLOCKS // 8
CHUNK = ROWS // 4
NBATCH = 2
AHEAD = 3
CHUNKS = ((0, 0, 16), (1, 0, 16), (0, 16, 16), (1, 16, 16), (0, 32, 16), (1, 32, 16), (0, 48, 16), (1, 48, 16))
FAR_FIRST = (4, 3, 5, 2, 6, 1, 7)


def split3(x):
    high = x.astype(BF16)
    rest = x - high.astype(F32)
    mid = rest.astype(BF16)
    low = (rest - mid.astype(F32)).astype(BF16)
    return high, mid, low


def dot(a, b):
    return jnp.dot(a, b, preferred_element_type=F32)


def table(kind, wide):
    shape = (LANES, 2 * LANES if wide else LANES)
    row = lax.broadcasted_iota(jnp.int32, shape, 0)
    col = lax.broadcasted_iota(jnp.int32, shape, 1)
    keep = {"ge": row >= col, "lt": row < col, "le": row <= col, "gt": row > col}[kind]
    if wide:
        keep = keep | (col >= LANES)
    return jnp.where(keep, 1.0, 0.0).astype(BF16)


def lane_scan(x, kind):
    wide = table(kind, True)
    high, mid, low = split3(x)
    both = dot(high, wide) + (dot(mid, wide) + dot(low, wide))
    return both[:, :LANES], both[:, LANES:]


def row_scan(totals, kind):
    side = table(kind, False)
    high, mid, low = split3(totals)
    return dot(side, high) + (dot(side, mid) + dot(side, low))


def pick(values, lanes):
    return jnp.take_along_axis(values, lanes, axis=1)


def fold(x):
    return x.reshape(BLOCKS // 8, 8, LANES).sum(axis=0)


def kernel(
    design, coefs, penalty, censor, codes, first, last,
    new_out, weights_out,
    D, C, PEN, CEN, COD, FST, LST, IC2, E, R1, R2, S, R4, ETA, EX, INV, BASE, TS, TR, W, SP, SR, SUM,
    load_sem, send_sem, recv_sem,
):
    s = lax.axis_index("subj")
    cov = lax.axis_index("cov")
    x = cov // RING
    z = cov % RING
    pos = (x, z)

    E5 = E.reshape(RING, RING, 2, BLOCKS, LANES)
    W5 = W.reshape(RING, RING, 2, BLOCKS, LANES)

    def device(axis, at):
        return (s, at * RING + z) if axis == 0 else (s, x * RING + at)

    def ring(axis):
        me = pos[axis]
        return (me + 3) % RING, (me + 1) % RING, (me + 2) % RING

    sent_rows = [0]
    groups = {}

    def rows_of(ref):
        size = 1
        for n in ref.shape[:-1]:
            size *= n
        return size * ref.shape[-1] // LANES

    def send(group, src, dst, to):
        at, rows = groups.get(group, (len(groups), 0))
        groups[group] = (at, rows + rows_of(src))
        sent_rows[0] += rows_of(src)
        pltpu.make_async_remote_copy(
            src_ref=src, dst_ref=dst, send_sem=send_sem.at[0], recv_sem=recv_sem.at[at],
            device_id=to, device_id_type=MESH,
        ).start()

    def wait_rows(sem, rows):
        span = W.at[pl.ds(0, rows), :]
        pltpu.make_async_copy(span, span, sem).wait()

    def received(*group):
        at, rows = groups[group]
        wait_rows(recv_sem.at[at], rows)

    barrier = pltpu.get_barrier_semaphore()
    peers = [device(axis, at) for axis in (0, 1) for at in ring(axis)]
    peers += [((s + d) % SUBJ, cov) for d in range(1, SUBJ)]
    for peer in peers:
        pl.semaphore_signal(barrier, inc=1, device_id=peer, device_id_type=MESH)

    chunks = []
    for i, (h, first_block, blocks) in enumerate(CHUNKS):
        part = pl.ds((h * HALF + first_block) * LANES, blocks * LANES)
        chunks.append(pltpu.make_async_copy(design.at[part], D.at[part], load_sem.at[i]))
    small = []
    for i, (src, dst) in enumerate(
        [(coefs, C), (penalty, PEN), (censor, CEN), (codes, COD), (first, FST), (last, LST)]
    ):
        small.append(pltpu.make_async_copy(src, dst, load_sem.at[len(CHUNKS) + i]))
    small[0].start()
    for copy in chunks[:AHEAD]:
        copy.start()

    small[0].wait()
    nt = (((1,), (1,)), ((), ()))
    lhs = C[...]

    def predict(h, first_block, blocks):
        start = (h * HALF + first_block) * LANES
        part = lax.dot_general(
            lhs, D[start : start + blocks * LANES, :], nt, preferred_element_type=F32
        )
        for j in range(blocks):
            block = h * HALF + first_block + j
            for g in range(4):
                E[pl.ds(g * 8 * BLOCKS + block, 8, stride=BLOCKS), :] = part[
                    g * 8 : g * 8 + 8, j * LANES : (j + 1) * LANES
                ]

    def quarter(ref, half, at, k, start, size):
        rows = pl.ds(half * HALF + start, size)
        return ref.at[at, :, k, rows, :] if half == 0 else ref.at[:, at, k, rows, :]

    def rs_far(h, k, part, d):
        left, right, opposite = ring(h)
        start = part * QUART + d * EIGHTH
        send(
            ("m1", h, k, part),
            quarter(E5, h, opposite, k, start, EIGHTH),
            R1.at[h, k, part, d],
            device(h, left if d else right),
        )

    def rs_near(h, k, part, d):
        left, right, opposite = ring(h)
        start = part * QUART + d * EIGHTH
        to = right if d else left
        send(
            ("m2", h, k, part),
            quarter(E5, h, to, k, start, EIGHTH),
            R2.at[h, k, 1 - d, :, pl.ds(start, EIGHTH), :],
            device(h, to),
        )

    def rs_on(h, k, part):
        left, right, opposite = ring(h)
        received("m1", h, k, part)
        for d, to in ((0, right), (1, left)):
            start = part * QUART + d * EIGHTH
            mine = quarter(E5, h, to, k, start, EIGHTH)
            mine[...] = mine[...] + R1[h, k, part, d]
            send(
                ("m2", h, k, part),
                mine,
                R2.at[h, k, d, :, pl.ds(start, EIGHTH), :],
                device(h, to),
            )

    def rs_second(h, k, part):
        received("m2", h, k, part)
        rows = pl.ds(part * QUART, QUART)
        S[h, k, :, rows, :] = (
            quarter(E5, h, pos[h], k, part * QUART, QUART)[...]
            + R2[h, k, 0, :, rows, :]
            + R2[h, k, 1, :, rows, :]
        )
        for slot, at in reversed(list(enumerate(ring(1 - h)))):
            send(("n", h, k), S.at[h, k, at, rows, :], R4.at[h, k, slot, rows, :], device(1 - h, at))

    def rs_end(h, k):
        received("n", h, k)
        ETA[k, pl.ds(h * HALF, HALF), :] = S[h, k, pos[1 - h]] + (
            R4[h, k, 0] + R4[h, k, 1] + R4[h, k, 2]
        )

    def exchange(k, e):
        for d in FAR_FIRST:
            send(("t", k, e), TS.at[k, e], TR.at[k, e, d], ((s + d) % SUBJ, cov))

    def arrived(k, e):
        received("t", k, e)
        after = jnp.zeros((8, LANES), F32)
        before = jnp.zeros((8, LANES), F32)
        for d in range(1, SUBJ):
            after = after + jnp.where(d > s, TR[k, e, d, 0], 0.0)
            before = before + jnp.where(d <= s, TR[k, e, d, 1], 0.0)
        return jnp.sum(after, keepdims=True), jnp.sum(before, keepdims=True)

    def prepare():
        for copy in small[1:]:
            copy.wait()
        FST[...] = FST[...] & (LANES - 1)
        LST[...] = LST[...] & (LANES - 1)
        IC2[...] = jnp.where(COD[...] == 2, 1.0 / CEN[...], 0.0)

    def scan_a(k):
        expo = jnp.exp(ETA[k])
        EX[k] = expo
        TS[k, 0, 0] = fold(expo)
        TS[k, 0, 1] = fold(expo * IC2[...])
        exchange(k, 0)

    def scan_a_local(k):
        expo = EX[k]
        risk, risk_rows = lane_scan(expo, "ge")
        before, before_rows = lane_scan(expo * IC2[...], "lt")
        lanes = FST[...]
        BASE[k] = (pick(risk, lanes) + row_scan(risk_rows, "lt")) + CEN[...] * (
            pick(before, lanes) + row_scan(before_rows, "gt")
        )

    def scan_b(k):
        risk_in, comp_in = arrived(k, 0)
        risk = BASE[k] + (risk_in + CEN[...] * comp_in)
        inv = jnp.where(COD[...] == 1, 1.0 / risk, 0.0)
        INV[k] = inv
        TS[k, 1, 0] = fold(inv * CEN[...])
        TS[k, 1, 1] = fold(inv)
        exchange(k, 1)

    def scan_b_local(k):
        inv = INV[k]
        upto, upto_rows = lane_scan(inv, "le")
        later, later_rows = lane_scan(inv * CEN[...], "gt")
        lanes = LST[...]
        BASE[k] = (pick(upto, lanes) + row_scan(upto_rows, "gt")) + IC2[...] * (
            pick(later, lanes) + row_scan(later_rows, "lt")
        )

    def scan_c(k):
        later_in, early_in = arrived(k, 1)
        event = jnp.where(COD[...] == 1, 1.0, 0.0)
        W5[x, z, k] = event - EX[k] * (BASE[k] + (early_in + IC2[...] * later_in))

    def ag_first(h, k, part):
        start = part * QUART
        rows = pl.ds(h * HALF + start, QUART)
        mine = W5.at[x, z, k, rows, :]
        for at in reversed(ring(1 - h)):
            send(("a1", h, k, part), mine, mine, device(1 - h, at))

    def ag_second(h, k, part):
        received("a1", h, k, part)
        left, right, opposite = ring(h)
        mine = quarter(W5, h, pos[h], k, part * QUART, QUART)
        for at in (left, right):
            send(("a2", h, k, part), mine, mine, device(h, at))

    def ag_third(h, k, part):
        left, right, opposite = ring(h)
        received("a2", h, k, part)
        for came, to, start in ((left, right, 0), (right, left, QUART // 2)):
            piece = quarter(W5, h, came, k, part * QUART + start, QUART // 2)
            send(("a3", h, k, part), piece, piece, device(h, to))

    def ag_end(h, k, part):
        received("a3", h, k, part)

    def score(k, part, total):
        def body(h, total):
            start = pl.multiple_of((2 * h + part) * CHUNK, CHUNK)
            parts = []
            for j in range(QUART):
                block = (2 * h + part) * QUART + j
                rows = [
                    W[pl.ds((g * 16 + k) * BLOCKS + block, 8, stride=2 * BLOCKS), :]
                    for g in range(2)
                ]
                parts.append(jnp.concatenate(rows, axis=0).astype(BF16))
            return total + dot(jnp.concatenate(parts, axis=1), D[pl.ds(start, CHUNK), :])

        return lax.fori_loop(0, 2, body, total)

    def score_out(k, total):
        SP[k] = total
        for d in FAR_FIRST:
            send(("s", k), SP.at[k], SR.at[k, s], ((s + d) % SUBJ, cov))
        SR[k, s] = total

    both = (0, 1)
    both = (0, 1)
    for i, (h, first_block, blocks) in enumerate(CHUNKS):
        chunks[i].wait()
        if i + AHEAD < len(chunks):
            chunks[i + AHEAD].start()
        elif i + AHEAD == len(chunks):
            for copy in small[1:]:
                copy.start()
        predict(h, first_block, blocks)
        if i == 0:
            pl.semaphore_wait(barrier, len(peers))
        for at in range(first_block // EIGHTH, (first_block + blocks) // EIGHTH):
            part, d = at // 2, at % 2
            rs_far(h, 0, part, d)
            rs_near(h, 0, part, d)
            rs_far(h, 1, part, d)
    for h in both:
        rs_on(h, 0, 0)
    for h in both:
        for d in both:
            rs_near(h, 1, 0, d)
    for h in both:
        rs_on(h, 0, 1)
    for h in both:
        for d in both:
            rs_near(h, 1, 1, d)
    prepare()
    for h in both:
        rs_on(h, 1, 0)
    for h in both:
        rs_second(h, 0, 0)
    for h in both:
        rs_on(h, 1, 1)
    for h in both:
        rs_second(h, 0, 1)
    for h in both:
        rs_second(h, 1, 0)
    for h in both:
        rs_second(h, 1, 1)
    for k in both:
        for h in both:
            rs_end(h, k)
        scan_a(k)
    for k in both:
        scan_a_local(k)
    for k in both:
        scan_b(k)
    for k in both:
        scan_b_local(k)
    for k in both:
        scan_c(k)
        for part in both:
            for h in both:
                ag_first(h, k, part)
    for step in (ag_second, ag_third):
        for k in both:
            for part in both:
                for h in both:
                    step(h, k, part)
    for k in both:
        total = jnp.zeros((PATHS // 2, COLS), F32)
        for part in both:
            for h in both:
                ag_end(h, k, part)
            total = score(k, part, total)
        score_out(k, total)

    def convert(block, carry):
        lanes = pl.ds(pl.multiple_of(block * LANES, LANES), LANES)
        for g in range(4):
            weights_out[g * 8 : g * 8 + 8, lanes] = W[
                pl.ds(g * 8 * BLOCKS + block, 8, stride=BLOCKS), :
            ]
        return carry

    lax.fori_loop(0, BLOCKS, convert, 0, unroll=8)
    eye = (
        lax.broadcasted_iota(jnp.int32, (PATHS, PATHS), 0)
        == lax.broadcasted_iota(jnp.int32, (PATHS, PATHS), 1)
    )
    limit = jnp.sum(
        jnp.where(eye, jnp.broadcast_to(PEN[...], (PATHS, PATHS)), 0.0), axis=1, keepdims=True
    )
    wide = C[...].astype(F32)
    for k in both:
        received("s", k)
        total = SR[k, 0]
        for i in range(1, SUBJ):
            total = total + SR[k, i]
        for c in range(2):
            SUM[c, pl.ds(k, PATHS // 2, stride=2), :] = total[:, c * LANES : (c + 1) * LANES]
    scale = 0.1 / jnp.sqrt(F32(SUBJ * ROWS))
    for c in range(2):
        cols = slice(c * LANES, (c + 1) * LANES)
        shifted = wide[:, cols] + scale * SUM[c]
        sign = jnp.where(shifted > 0, 1.0, jnp.where(shifted < 0, -1.0, 0.0))
        new_out[:, cols] = sign * jnp.maximum(jnp.abs(shifted) - limit, 0.0)
    left_rows = sent_rows[0]
    span = D.at[pl.ds(0, left_rows), :]
    pltpu.make_async_copy(span, span, send_sem.at[0]).wait()


def hand_over(new, weights, new_out, weights_out, sem):
    copies = [pltpu.make_async_copy(new, new_out, sem.at[4])]
    for c in range(4):
        rows = pl.ds(c * 8, 8)
        copies.append(pltpu.make_async_copy(weights.at[rows], weights_out.at[rows], sem.at[c]))
    for copy in copies:
        copy.start()
    for copy in copies:
        copy.wait()


def local(design, coefs, penalty, censor, codes, tie_first, tie_last):
    square = (BLOCKS, LANES)
    vmem = pltpu.VMEM
    dma = pltpu.SemaphoreType.DMA
    new, weights = pl.pallas_call(
        kernel,
        out_shape=(
            jax.ShapeDtypeStruct((PATHS, COLS), F32),
            jax.ShapeDtypeStruct((PATHS, ROWS), F32),
        ),
        in_specs=[pl.BlockSpec(memory_space=pltpu.HBM)] * 7,
        out_specs=(pl.BlockSpec(memory_space=pltpu.VMEM), pl.BlockSpec(memory_space=pltpu.VMEM)),
        scratch_shapes=[
            vmem((ROWS, COLS), BF16),
            vmem((PATHS, COLS), BF16),
            vmem((1, PATHS), F32),
            vmem(square, F32),
            vmem(square, jnp.int32),
            vmem(square, jnp.int32),
            vmem(square, jnp.int32),
            vmem(square, F32),
            vmem((PATHS * BLOCKS, LANES), F32),
            vmem((2, NBATCH, 2, 2, RING, EIGHTH, LANES), F32),
            vmem((2, NBATCH, 2, RING, HALF, LANES), F32),
            vmem((2, NBATCH, RING, HALF, LANES), F32),
            vmem((2, NBATCH, 3, HALF, LANES), F32),
            vmem((NBATCH, BLOCKS, LANES), F32),
            vmem((NBATCH, BLOCKS, LANES), F32),
            vmem((NBATCH, BLOCKS, LANES), F32),
            vmem((NBATCH, BLOCKS, LANES), F32),
            vmem((NBATCH, 2, 2, 8, LANES), F32),
            vmem((NBATCH, 2, SUBJ, 2, 8, LANES), F32),
            vmem((PATHS * BLOCKS, LANES), F32),
            vmem((NBATCH, PATHS // 2, COLS), F32),
            vmem((NBATCH, SUBJ, PATHS // 2, COLS), F32),
            vmem((2, PATHS, LANES), F32),
            dma((len(CHUNKS) + 6,)),
            dma((1,)),
            dma((50,)),
        ],
        compiler_params=pltpu.CompilerParams(
            collective_id=0, has_side_effects=True, vmem_limit_bytes=48 * 2**20
        ),
        cost_estimate=pl.CostEstimate(
            flops=4 * PATHS * ROWS * COLS,
            bytes_accessed=2 * ROWS * COLS + 4 * PATHS * ROWS,
            transcendentals=2 * ROWS,
        ),
    )(
        *(
            pltpu.with_memory_space_constraint(a, pltpu.HBM)
            for a in (
                design,
                coefs.T,
                penalty.reshape(1, PATHS),
                censor.reshape(square),
                codes.reshape(square),
                tie_first.reshape(square),
                tie_last.reshape(square),
            )
        )
    )
    new, weights = pl.pallas_call(
        hand_over,
        out_shape=(
            jax.ShapeDtypeStruct((PATHS, COLS), F32),
            jax.ShapeDtypeStruct((PATHS, ROWS), F32),
        ),
        in_specs=[pl.BlockSpec(memory_space=pltpu.VMEM)] * 2,
        out_specs=(pl.BlockSpec(memory_space=pltpu.HBM), pl.BlockSpec(memory_space=pltpu.HBM)),
        scratch_shapes=[dma((5,))],
        compiler_params=pltpu.CompilerParams(vmem_limit_bytes=40 * 2**20),
    )(new, weights)
    return new.T, weights


def solution(mesh):
    in_specs = (P("subj", "cov"), P("cov", None), P(), P("subj"), P("subj"), P("subj"), P("subj"))
    out_specs = (P("cov", None), P(None, "subj"))
    return jax.shard_map(local, mesh=mesh, in_specs=in_specs, out_specs=out_specs, check_vma=False)
```

```python
import functools

import jax
import jax.numpy as jnp
from jax import lax
from jax.experimental import pallas as pl
from jax.experimental.pallas import tpu as pltpu
from jax.sharding import PartitionSpec as P

MESH = pl.DeviceIdType.MESH
F32 = jnp.float32
BF16 = jnp.bfloat16
LANES = 128
SUBJ = 8
RING = 4
PATHS = 32
ROWS = 16384
COLS = 256
BLOCKS = ROWS // LANES
HALF = BLOCKS // 2
QUART = BLOCKS // 4
EIGHTH = BLOCKS // 8
CHUNK = ROWS // 4
NBATCH = 2
AHEAD = 3
CHUNKS = ((0, 0, 16), (1, 0, 16), (0, 16, 16), (1, 16, 16), (0, 32, 16), (1, 32, 16), (0, 48, 16), (1, 48, 16))
FAR_FIRST = (4, 3, 5, 2, 6, 1, 7)


def split3(x):
    high = x.astype(BF16)
    rest = x - high.astype(F32)
    mid = rest.astype(BF16)
    low = (rest - mid.astype(F32)).astype(BF16)
    return high, mid, low


def dot(a, b):
    return jnp.dot(a, b, preferred_element_type=F32)


def table(kind, wide):
    shape = (LANES, 2 * LANES if wide else LANES)
    row = lax.broadcasted_iota(jnp.int32, shape, 0)
    col = lax.broadcasted_iota(jnp.int32, shape, 1)
    keep = {"ge": row >= col, "lt": row < col, "le": row <= col, "gt": row > col}[kind]
    if wide:
        keep = keep | (col >= LANES)
    return jnp.where(keep, 1.0, 0.0).astype(BF16)


def lane_scan(x, kind):
    wide = table(kind, True)
    high, mid, low = split3(x)
    both = dot(high, wide) + (dot(mid, wide) + dot(low, wide))
    return both[:, :LANES], both[:, LANES:]


def row_scan(totals, kind):
    side = table(kind, False)
    high, mid, low = split3(totals)
    return dot(side, high) + (dot(side, mid) + dot(side, low))


def pick(values, lanes):
    return jnp.take_along_axis(values, lanes, axis=1)


def fold(x):
    return x.reshape(BLOCKS // 8, 8, LANES).sum(axis=0)


def kernel(
    design, coefs, penalty, censor, codes, first, last,
    new_out, weights_out,
    D, C, PEN, CEN, COD, FST, LST, IC2, E, R1, R2, S, R4, ETA, EX, INV, BASE, TS, TR, W, SP, SR, SUM,
    load_sem, send_sem, recv_sem,
):
    s = lax.axis_index("subj")
    cov = lax.axis_index("cov")
    x = cov // RING
    z = cov % RING
    pos = (x, z)

    E5 = E.at[pl.ds(0, PATHS * BLOCKS)].reshape(RING, RING, 2, BLOCKS, LANES)
    W5 = W.at[pl.ds(0, PATHS * BLOCKS)].reshape(RING, RING, 2, BLOCKS, LANES)

    def device(axis, at):
        return (s, at * RING + z) if axis == 0 else (s, x * RING + at)

    def ring(axis):
        me = pos[axis]
        return (me + 3) % RING, (me + 1) % RING, (me + 2) % RING

    sent_rows = [0]
    groups = {}

    def rows_of(ref):
        size = 1
        for n in ref.shape[:-1]:
            size *= n
        return size * ref.shape[-1] // LANES

    def send(group, src, dst, to):
        at, rows = groups.get(group, (len(groups), 0))
        groups[group] = (at, rows + rows_of(src))
        sent_rows[0] += rows_of(src)
        pltpu.make_async_remote_copy(
            src_ref=src, dst_ref=dst, send_sem=send_sem.at[0], recv_sem=recv_sem.at[at],
            device_id=to, device_id_type=MESH,
        ).start()

    def wait_rows(sem, rows):
        span = W.at[pl.ds(0, rows), :]
        pltpu.make_async_copy(span, span, sem).wait()

    def received(*group):
        at, rows = groups[group]
        wait_rows(recv_sem.at[at], rows)

    barrier = pltpu.get_barrier_semaphore()
    peers = [device(axis, at) for axis in (0, 1) for at in ring(axis)]
    peers += [((s + d) % SUBJ, cov) for d in range(1, SUBJ)]
    for peer in peers:
        pl.semaphore_signal(barrier, inc=1, device_id=peer, device_id_type=MESH)

    chunks = []
    for i, (h, first_block, blocks) in enumerate(CHUNKS):
        part = pl.ds((h * HALF + first_block) * LANES, blocks * LANES)
        chunks.append(pltpu.make_async_copy(design.at[part], D.at[part], load_sem.at[i]))
    small = []
    for i, (src, dst) in enumerate(
        [(coefs, C), (penalty, PEN), (censor, CEN), (codes, COD), (first, FST), (last, LST)]
    ):
        small.append(pltpu.make_async_copy(src, dst, load_sem.at[len(CHUNKS) + i]))
    small[0].start()
    for copy in chunks[:AHEAD]:
        copy.start()

    small[0].wait()
    nt = (((1,), (1,)), ((), ()))
    lhs = C[...]

    def predict(h, first_block, blocks):
        start = (h * HALF + first_block) * LANES
        part = lax.dot_general(
            lhs, D[start : start + blocks * LANES, :], nt, preferred_element_type=F32
        )
        for j in range(blocks):
            block = h * HALF + first_block + j
            for g in range(4):
                E[pl.ds(g * 8 * BLOCKS + block, 8, stride=BLOCKS), :] = part[
                    g * 8 : g * 8 + 8, j * LANES : (j + 1) * LANES
                ]

    def quarter(ref, half, at, k, start, size):
        rows = pl.ds(half * HALF + start, size)
        return ref.at[at, :, k, rows, :] if half == 0 else ref.at[:, at, k, rows, :]

    def rs_far(h, k, part, d):
        left, right, opposite = ring(h)
        start = part * QUART + d * EIGHTH
        send(
            ("m1", h, k, part),
            quarter(E5, h, opposite, k, start, EIGHTH),
            R1.at[h, k, part, d],
            device(h, left if d else right),
        )

    def rs_near(h, k, part, d):
        left, right, opposite = ring(h)
        start = part * QUART + d * EIGHTH
        to = right if d else left
        send(
            ("m2", h, k, part),
            quarter(E5, h, to, k, start, EIGHTH),
            R2.at[h, k, 1 - d, :, pl.ds(start, EIGHTH), :],
            device(h, to),
        )

    def rs_on(h, k, part):
        left, right, opposite = ring(h)
        received("m1", h, k, part)
        for d, to in ((0, right), (1, left)):
            start = part * QUART + d * EIGHTH
            mine = quarter(E5, h, to, k, start, EIGHTH)
            mine[...] = mine[...] + R1[h, k, part, d]
            send(
                ("m2", h, k, part),
                mine,
                R2.at[h, k, d, :, pl.ds(start, EIGHTH), :],
                device(h, to),
            )

    def rs_second(h, k, part):
        received("m2", h, k, part)
        rows = pl.ds(part * QUART, QUART)
        S[h, k, :, rows, :] = (
            quarter(E5, h, pos[h], k, part * QUART, QUART)[...]
            + R2[h, k, 0, :, rows, :]
            + R2[h, k, 1, :, rows, :]
        )
        for slot, at in reversed(list(enumerate(ring(1 - h)))):
            send(("n", h, k), S.at[h, k, at, rows, :], R4.at[h, k, slot, rows, :], device(1 - h, at))

    def rs_end(h, k):
        received("n", h, k)
        ETA[k, pl.ds(h * HALF, HALF), :] = S[h, k, pos[1 - h]] + (
            R4[h, k, 0] + R4[h, k, 1] + R4[h, k, 2]
        )

    def exchange(k, e):
        for d in FAR_FIRST:
            send(("t", k, e), TS.at[k, e], TR.at[k, e, d], ((s + d) % SUBJ, cov))

    def arrived(k, e):
        received("t", k, e)
        after = jnp.zeros((8, LANES), F32)
        before = jnp.zeros((8, LANES), F32)
        for d in range(1, SUBJ):
            after = after + jnp.where(d > s, TR[k, e, d, 0], 0.0)
            before = before + jnp.where(d <= s, TR[k, e, d, 1], 0.0)
        return jnp.sum(after, keepdims=True), jnp.sum(before, keepdims=True)

    def prepare():
        for copy in small[1:]:
            copy.wait()
        FST[...] = FST[...] & (LANES - 1)
        LST[...] = LST[...] & (LANES - 1)
        IC2[...] = jnp.where(COD[...] == 2, 1.0 / CEN[...], 0.0)

    def scan_a(k):
        expo = jnp.exp(ETA[k])
        EX[k] = expo
        TS[k, 0, 0] = fold(expo)
        TS[k, 0, 1] = fold(expo * IC2[...])
        exchange(k, 0)

    def scan_a_local(k):
        expo = EX[k]
        risk, risk_rows = lane_scan(expo, "ge")
        before, before_rows = lane_scan(expo * IC2[...], "lt")
        lanes = FST[...]
        BASE[k] = (pick(risk, lanes) + row_scan(risk_rows, "lt")) + CEN[...] * (
            pick(before, lanes) + row_scan(before_rows, "gt")
        )

    def scan_b(k):
        risk_in, comp_in = arrived(k, 0)
        risk = BASE[k] + (risk_in + CEN[...] * comp_in)
        inv = jnp.where(COD[...] == 1, 1.0 / risk, 0.0)
        INV[k] = inv
        TS[k, 1, 0] = fold(inv * CEN[...])
        TS[k, 1, 1] = fold(inv)
        exchange(k, 1)

    def scan_b_local(k):
        inv = INV[k]
        upto, upto_rows = lane_scan(inv, "le")
        later, later_rows = lane_scan(inv * CEN[...], "gt")
        lanes = LST[...]
        BASE[k] = (pick(upto, lanes) + row_scan(upto_rows, "gt")) + IC2[...] * (
            pick(later, lanes) + row_scan(later_rows, "lt")
        )

    def scan_c(k):
        later_in, early_in = arrived(k, 1)
        event = jnp.where(COD[...] == 1, 1.0, 0.0)
        W5[x, z, k] = event - EX[k] * (BASE[k] + (early_in + IC2[...] * later_in))

    def ag_first(h, k, part):
        start = part * QUART
        rows = pl.ds(h * HALF + start, QUART)
        mine = W5.at[x, z, k, rows, :]
        for at in reversed(ring(1 - h)):
            send(("a1", h, k, part), mine, mine, device(1 - h, at))

    def ag_second(h, k, part):
        received("a1", h, k, part)
        left, right, opposite = ring(h)
        mine = quarter(W5, h, pos[h], k, part * QUART, QUART)
        for at in (left, right):
            send(("a2", h, k, part), mine, mine, device(h, at))

    def ag_third(h, k, part):
        left, right, opposite = ring(h)
        received("a2", h, k, part)
        for came, to, start in ((left, right, 0), (right, left, QUART // 2)):
            piece = quarter(W5, h, came, k, part * QUART + start, QUART // 2)
            send(("a3", h, k, part), piece, piece, device(h, to))

    def ag_end(h, k, part):
        received("a3", h, k, part)

    def score(k, part, total):
        def body(h, total):
            start = pl.multiple_of((2 * h + part) * CHUNK, CHUNK)
            parts = []
            for j in range(QUART):
                block = (2 * h + part) * QUART + j
                rows = [
                    W[pl.ds((g * 16 + k) * BLOCKS + block, 8, stride=2 * BLOCKS), :]
                    for g in range(2)
                ]
                parts.append(jnp.concatenate(rows, axis=0).astype(BF16))
            return total + dot(jnp.concatenate(parts, axis=1), D[pl.ds(start, CHUNK), :])

        return lax.fori_loop(0, 2, body, total)

    def score_out(k, total):
        SP[k] = total
        for d in FAR_FIRST:
            send(("s", k), SP.at[k], SR.at[k, s], ((s + d) % SUBJ, cov))
        SR[k, s] = total

    both = (0, 1)
    both = (0, 1)
    for i, (h, first_block, blocks) in enumerate(CHUNKS):
        chunks[i].wait()
        if i + AHEAD < len(chunks):
            chunks[i + AHEAD].start()
        elif i + AHEAD == len(chunks):
            for copy in small[1:]:
                copy.start()
        predict(h, first_block, blocks)
        if i == 0:
            pl.semaphore_wait(barrier, len(peers))
        for at in range(first_block // EIGHTH, (first_block + blocks) // EIGHTH):
            part, d = at // 2, at % 2
            rs_far(h, 0, part, d)
            rs_near(h, 0, part, d)
            rs_far(h, 1, part, d)
    for h in both:
        rs_on(h, 0, 0)
    for h in both:
        for d in both:
            rs_near(h, 1, 0, d)
    for h in both:
        rs_on(h, 0, 1)
    for h in both:
        for d in both:
            rs_near(h, 1, 1, d)
    for h in both:
        rs_on(h, 1, 0)
    for h in both:
        rs_second(h, 0, 0)
    for h in both:
        rs_on(h, 1, 1)
    for h in both:
        rs_second(h, 0, 1)
    for h in both:
        rs_second(h, 1, 0)
    for h in both:
        rs_second(h, 1, 1)
    prepare()
    for k in both:
        for h in both:
            rs_end(h, k)
        scan_a(k)
    for k in both:
        scan_a_local(k)
    for k in both:
        scan_b(k)
    for k in both:
        scan_b_local(k)
    for k in both:
        scan_c(k)
        for part in both:
            for h in both:
                ag_first(h, k, part)
    for step in (ag_second, ag_third):
        for k in both:
            for part in both:
                for h in both:
                    step(h, k, part)
    for k in both:
        total = jnp.zeros((PATHS // 2, COLS), F32)
        for part in both:
            for h in both:
                ag_end(h, k, part)
            total = score(k, part, total)
        score_out(k, total)

    def convert(block, carry):
        lanes = pl.ds(pl.multiple_of(block * LANES, LANES), LANES)
        for g in range(4):
            weights_out[g * 8 : g * 8 + 8, lanes] = W[
                pl.ds(g * 8 * BLOCKS + block, 8, stride=BLOCKS), :
            ]
        return carry

    lax.fori_loop(0, BLOCKS, convert, 0, unroll=8)
    eye = (
        lax.broadcasted_iota(jnp.int32, (PATHS, PATHS), 0)
        == lax.broadcasted_iota(jnp.int32, (PATHS, PATHS), 1)
    )
    limit = jnp.sum(
        jnp.where(eye, jnp.broadcast_to(PEN[...], (PATHS, PATHS)), 0.0), axis=1, keepdims=True
    )
    wide = C[...].astype(F32)
    for k in both:
        received("s", k)
        total = SR[k, 0]
        for i in range(1, SUBJ):
            total = total + SR[k, i]
        for c in range(2):
            SUM[c, pl.ds(k, PATHS // 2, stride=2), :] = total[:, c * LANES : (c + 1) * LANES]
    scale = 0.1 / jnp.sqrt(F32(SUBJ * ROWS))
    for c in range(2):
        cols = slice(c * LANES, (c + 1) * LANES)
        shifted = wide[:, cols] + scale * SUM[c, 0:PATHS, :]
        sign = jnp.where(shifted > 0, 1.0, jnp.where(shifted < 0, -1.0, 0.0))
        new_out[:, cols] = sign * jnp.maximum(jnp.abs(shifted) - limit, 0.0)
    left_rows = sent_rows[0]
    span = D.at[pl.ds(0, left_rows), :]
    pltpu.make_async_copy(span, span, send_sem.at[0]).wait()


def hand_over(new, weights, new_out, weights_out, sem):
    copies = [pltpu.make_async_copy(new, new_out, sem.at[4])]
    for c in range(4):
        rows = pl.ds(c * 8, 8)
        copies.append(pltpu.make_async_copy(weights.at[rows], weights_out.at[rows], sem.at[c]))
    for copy in copies:
        copy.start()
    for copy in copies:
        copy.wait()


def local(design, coefs, penalty, censor, codes, tie_first, tie_last):
    square = (BLOCKS, LANES)
    vmem = pltpu.VMEM
    dma = pltpu.SemaphoreType.DMA
    new, weights = pl.pallas_call(
        kernel,
        out_shape=(
            jax.ShapeDtypeStruct((PATHS, COLS), F32),
            jax.ShapeDtypeStruct((PATHS, ROWS), F32),
        ),
        in_specs=[pl.BlockSpec(memory_space=pltpu.HBM)] * 7,
        out_specs=(pl.BlockSpec(memory_space=pltpu.VMEM), pl.BlockSpec(memory_space=pltpu.VMEM)),
        scratch_shapes=[
            vmem((ROWS, COLS), BF16),
            vmem((PATHS, COLS), BF16),
            vmem((1, PATHS), F32),
            vmem(square, F32),
            vmem(square, jnp.int32),
            vmem(square, jnp.int32),
            vmem(square, jnp.int32),
            vmem(square, F32),
            vmem((PATHS * BLOCKS + BLOCKS, LANES), F32),
            vmem((2, NBATCH, 2, 2, RING, EIGHTH, LANES), F32),
            vmem((2, NBATCH, 2, RING, HALF, LANES), F32),
            vmem((2, NBATCH, RING, HALF, LANES), F32),
            vmem((2, NBATCH, 3, HALF, LANES), F32),
            vmem((NBATCH, BLOCKS, LANES), F32),
            vmem((NBATCH, BLOCKS, LANES), F32),
            vmem((NBATCH, BLOCKS, LANES), F32),
            vmem((NBATCH, BLOCKS, LANES), F32),
            vmem((NBATCH, 2, 2, 8, LANES), F32),
            vmem((NBATCH, 2, SUBJ, 2, 8, LANES), F32),
            vmem((PATHS * BLOCKS + 2 * BLOCKS, LANES), F32),
            vmem((NBATCH, PATHS // 2, COLS), F32),
            vmem((NBATCH, SUBJ, PATHS // 2, COLS), F32),
            vmem((2, PATHS + 8, LANES), F32),
            dma((len(CHUNKS) + 6,)),
            dma((1,)),
            dma((50,)),
        ],
        compiler_params=pltpu.CompilerParams(
            collective_id=0, has_side_effects=True, vmem_limit_bytes=48 * 2**20
        ),
        cost_estimate=pl.CostEstimate(
            flops=4 * PATHS * ROWS * COLS,
            bytes_accessed=2 * ROWS * COLS + 4 * PATHS * ROWS,
            transcendentals=2 * ROWS,
        ),
    )(
        *(
            pltpu.with_memory_space_constraint(a, pltpu.HBM)
            for a in (
                design,
                coefs.T,
                penalty.reshape(1, PATHS),
                censor.reshape(square),
                codes.reshape(square),
                tie_first.reshape(square),
                tie_last.reshape(square),
            )
        )
    )
    new, weights = pl.pallas_call(
        hand_over,
        out_shape=(
            jax.ShapeDtypeStruct((PATHS, COLS), F32),
            jax.ShapeDtypeStruct((PATHS, ROWS), F32),
        ),
        in_specs=[pl.BlockSpec(memory_space=pltpu.VMEM)] * 2,
        out_specs=(pl.BlockSpec(memory_space=pltpu.HBM), pl.BlockSpec(memory_space=pltpu.HBM)),
        scratch_shapes=[dma((5,))],
        compiler_params=pltpu.CompilerParams(vmem_limit_bytes=40 * 2**20),
    )(new, weights)
    return new.T, weights


def solution(mesh):
    in_specs = (P("subj", "cov"), P("cov", None), P(), P("subj"), P("subj"), P("subj"), P("subj"))
    out_specs = (P("cov", None), P(None, "subj"))
    return jax.shard_map(local, mesh=mesh, in_specs=in_specs, out_specs=out_specs, check_vma=False)
```

```python
import functools

import jax
import jax.numpy as jnp
from jax import lax
from jax.experimental import pallas as pl
from jax.experimental.pallas import tpu as pltpu
from jax.sharding import PartitionSpec as P

MESH = pl.DeviceIdType.MESH
F32 = jnp.float32
BF16 = jnp.bfloat16
LANES = 128
SUBJ = 8
RING = 4
PATHS = 32
ROWS = 16384
COLS = 256
BLOCKS = ROWS // LANES
HALF = BLOCKS // 2
QUART = BLOCKS // 4
EIGHTH = BLOCKS // 8
CHUNK = ROWS // 4
NBATCH = 2
AHEAD = 4
CHUNKS = ((0, 0, 16), (1, 0, 16), (0, 16, 16), (1, 16, 16), (0, 32, 16), (1, 32, 16), (0, 48, 16), (1, 48, 16))
FAR_FIRST = (4, 3, 5, 2, 6, 1, 7)


def split3(x):
    high = x.astype(BF16)
    rest = x - high.astype(F32)
    mid = rest.astype(BF16)
    low = (rest - mid.astype(F32)).astype(BF16)
    return high, mid, low


def dot(a, b):
    return jnp.dot(a, b, preferred_element_type=F32)


def table(kind, wide):
    shape = (LANES, 2 * LANES if wide else LANES)
    row = lax.broadcasted_iota(jnp.int32, shape, 0)
    col = lax.broadcasted_iota(jnp.int32, shape, 1)
    keep = {"ge": row >= col, "lt": row < col, "le": row <= col, "gt": row > col}[kind]
    if wide:
        keep = keep | (col >= LANES)
    return jnp.where(keep, 1.0, 0.0).astype(BF16)


def lane_scan(x, kind):
    wide = table(kind, True)
    high, mid, low = split3(x)
    both = dot(high, wide) + (dot(mid, wide) + dot(low, wide))
    return both[:, :LANES], both[:, LANES:]


def row_scan(totals, kind):
    side = table(kind, False)
    high, mid, low = split3(totals)
    return dot(side, high) + (dot(side, mid) + dot(side, low))


def pick(values, lanes):
    return jnp.take_along_axis(values, lanes, axis=1)


def fold(x):
    return x.reshape(BLOCKS // 8, 8, LANES).sum(axis=0)


def kernel(
    design, coefs, penalty, censor, codes, first, last,
    new_out, weights_out,
    D, C, PEN, CEN, COD, FST, LST, IC2, E, R1, R2, S, R4, ETA, EX, INV, BASE, TS, TR, W, SP, SR, SUM,
    load_sem, send_sem, recv_sem,
):
    s = lax.axis_index("subj")
    cov = lax.axis_index("cov")
    x = cov // RING
    z = cov % RING
    pos = (x, z)

    E5 = E.at[pl.ds(0, PATHS * BLOCKS)].reshape(RING, RING, 2, BLOCKS, LANES)
    W5 = W.at[pl.ds(0, PATHS * BLOCKS)].reshape(RING, RING, 2, BLOCKS, LANES)

    def device(axis, at):
        return (s, at * RING + z) if axis == 0 else (s, x * RING + at)

    def ring(axis):
        me = pos[axis]
        return (me + 3) % RING, (me + 1) % RING, (me + 2) % RING

    sent_rows = [0]
    groups = {}

    def rows_of(ref):
        size = 1
        for n in ref.shape[:-1]:
            size *= n
        return size * ref.shape[-1] // LANES

    def send(group, src, dst, to):
        at, rows = groups.get(group, (len(groups), 0))
        groups[group] = (at, rows + rows_of(src))
        sent_rows[0] += rows_of(src)
        pltpu.make_async_remote_copy(
            src_ref=src, dst_ref=dst, send_sem=send_sem.at[0], recv_sem=recv_sem.at[at],
            device_id=to, device_id_type=MESH,
        ).start()

    def wait_rows(sem, rows):
        span = W.at[pl.ds(0, rows), :]
        pltpu.make_async_copy(span, span, sem).wait()

    def received(*group):
        at, rows = groups[group]
        wait_rows(recv_sem.at[at], rows)

    barrier = pltpu.get_barrier_semaphore()
    peers = [device(axis, at) for axis in (0, 1) for at in ring(axis)]
    peers += [((s + d) % SUBJ, cov) for d in range(1, SUBJ)]
    for peer in peers:
        pl.semaphore_signal(barrier, inc=1, device_id=peer, device_id_type=MESH)

    chunks = []
    for i, (h, first_block, blocks) in enumerate(CHUNKS):
        part = pl.ds((h * HALF + first_block) * LANES, blocks * LANES)
        chunks.append(pltpu.make_async_copy(design.at[part], D.at[part], load_sem.at[i]))
    small = []
    for i, (src, dst) in enumerate(
        [(coefs, C), (penalty, PEN), (censor, CEN), (codes, COD), (first, FST), (last, LST)]
    ):
        small.append(pltpu.make_async_copy(src, dst, load_sem.at[len(CHUNKS) + i]))
    small[0].start()
    for copy in chunks[:AHEAD]:
        copy.start()

    small[0].wait()
    nt = (((1,), (1,)), ((), ()))
    lhs = C[...]

    def predict(h, first_block, blocks):
        start = (h * HALF + first_block) * LANES
        part = lax.dot_general(
            lhs, D[start : start + blocks * LANES, :], nt, preferred_element_type=F32
        )
        for j in range(blocks):
            block = h * HALF + first_block + j
            for g in range(4):
                E[pl.ds(g * 8 * BLOCKS + block, 8, stride=BLOCKS), :] = part[
                    g * 8 : g * 8 + 8, j * LANES : (j + 1) * LANES
                ]

    def quarter(ref, half, at, k, start, size):
        rows = pl.ds(half * HALF + start, size)
        return ref.at[at, :, k, rows, :] if half == 0 else ref.at[:, at, k, rows, :]

    def rs_far(h, k, part, d):
        left, right, opposite = ring(h)
        start = part * QUART + d * EIGHTH
        send(
            ("m1", h, k, part),
            quarter(E5, h, opposite, k, start, EIGHTH),
            R1.at[h, k, part, d],
            device(h, left if d else right),
        )

    def rs_near(h, k, part, d):
        left, right, opposite = ring(h)
        start = part * QUART + d * EIGHTH
        to = right if d else left
        send(
            ("m2", h, k, part),
            quarter(E5, h, to, k, start, EIGHTH),
            R2.at[h, k, 1 - d, :, pl.ds(start, EIGHTH), :],
            device(h, to),
        )

    def rs_on(h, k, part):
        left, right, opposite = ring(h)
        received("m1", h, k, part)
        for d, to in ((0, right), (1, left)):
            start = part * QUART + d * EIGHTH
            mine = quarter(E5, h, to, k, start, EIGHTH)
            mine[...] = mine[...] + R1[h, k, part, d]
            send(
                ("m2", h, k, part),
                mine,
                R2.at[h, k, d, :, pl.ds(start, EIGHTH), :],
                device(h, to),
            )

    def rs_second(h, k, part):
        received("m2", h, k, part)
        rows = pl.ds(part * QUART, QUART)
        S[h, k, :, rows, :] = (
            quarter(E5, h, pos[h], k, part * QUART, QUART)[...]
            + R2[h, k, 0, :, rows, :]
            + R2[h, k, 1, :, rows, :]
        )
        for slot, at in reversed(list(enumerate(ring(1 - h)))):
            send(("n", h, k), S.at[h, k, at, rows, :], R4.at[h, k, slot, rows, :], device(1 - h, at))

    def rs_end(h, k):
        received("n", h, k)
        ETA[k, pl.ds(h * HALF, HALF), :] = S[h, k, pos[1 - h]] + (
            R4[h, k, 0] + R4[h, k, 1] + R4[h, k, 2]
        )

    def exchange(k, e):
        for d in FAR_FIRST:
            send(("t", k, e), TS.at[k, e], TR.at[k, e, d], ((s + d) % SUBJ, cov))

    def arrived(k, e):
        received("t", k, e)
        after = jnp.zeros((8, LANES), F32)
        before = jnp.zeros((8, LANES), F32)
        for d in range(1, SUBJ):
            after = after + jnp.where(d > s, TR[k, e, d, 0], 0.0)
            before = before + jnp.where(d <= s, TR[k, e, d, 1], 0.0)
        return jnp.sum(after, keepdims=True), jnp.sum(before, keepdims=True)

    def prepare():
        for copy in small[1:]:
            copy.wait()
        FST[...] = FST[...] & (LANES - 1)
        LST[...] = LST[...] & (LANES - 1)
        IC2[...] = jnp.where(COD[...] == 2, 1.0 / CEN[...], 0.0)

    def scan_a(k):
        expo = jnp.exp(ETA[k])
        EX[k] = expo
        TS[k, 0, 0] = fold(expo)
        TS[k, 0, 1] = fold(expo * IC2[...])
        exchange(k, 0)

    def scan_a_local(k):
        expo = EX[k]
        risk, risk_rows = lane_scan(expo, "ge")
        before, before_rows = lane_scan(expo * IC2[...], "lt")
        lanes = FST[...]
        BASE[k] = (pick(risk, lanes) + row_scan(risk_rows, "lt")) + CEN[...] * (
            pick(before, lanes) + row_scan(before_rows, "gt")
        )

    def scan_b(k):
        risk_in, comp_in = arrived(k, 0)
        risk = BASE[k] + (risk_in + CEN[...] * comp_in)
        inv = jnp.where(COD[...] == 1, 1.0 / risk, 0.0)
        INV[k] = inv
        TS[k, 1, 0] = fold(inv * CEN[...])
        TS[k, 1, 1] = fold(inv)
        exchange(k, 1)

    def scan_b_local(k):
        inv = INV[k]
        upto, upto_rows = lane_scan(inv, "le")
        later, later_rows = lane_scan(inv * CEN[...], "gt")
        lanes = LST[...]
        BASE[k] = (pick(upto, lanes) + row_scan(upto_rows, "gt")) + IC2[...] * (
            pick(later, lanes) + row_scan(later_rows, "lt")
        )

    def scan_c(k):
        later_in, early_in = arrived(k, 1)
        event = jnp.where(COD[...] == 1, 1.0, 0.0)
        W5[x, z, k] = event - EX[k] * (BASE[k] + (early_in + IC2[...] * later_in))

    def ag_first(h, k, part):
        start = part * QUART
        rows = pl.ds(h * HALF + start, QUART)
        mine = W5.at[x, z, k, rows, :]
        for at in reversed(ring(1 - h)):
            send(("a1", h, k, part), mine, mine, device(1 - h, at))

    def ag_second(h, k, part):
        received("a1", h, k, part)
        left, right, opposite = ring(h)
        mine = quarter(W5, h, pos[h], k, part * QUART, QUART)
        for at in (left, right):
            send(("a2", h, k, part), mine, mine, device(h, at))

    def ag_third(h, k, part):
        left, right, opposite = ring(h)
        received("a2", h, k, part)
        for came, to, start in ((left, right, 0), (right, left, QUART // 2)):
            piece = quarter(W5, h, came, k, part * QUART + start, QUART // 2)
            send(("a3", h, k, part), piece, piece, device(h, to))

    def ag_end(h, k, part):
        received("a3", h, k, part)

    def score(k, part, total):
        def body(h, total):
            start = pl.multiple_of((2 * h + part) * CHUNK, CHUNK)
            parts = []
            for j in range(QUART):
                block = (2 * h + part) * QUART + j
                rows = [
                    W[pl.ds((g * 16 + k) * BLOCKS + block, 8, stride=2 * BLOCKS), :]
                    for g in range(2)
                ]
                parts.append(jnp.concatenate(rows, axis=0).astype(BF16))
            return total + dot(jnp.concatenate(parts, axis=1), D[pl.ds(start, CHUNK), :])

        return lax.fori_loop(0, 2, body, total)

    def score_out(k, total):
        SP[k] = total
        for d in FAR_FIRST:
            send(("s", k), SP.at[k], SR.at[k, s], ((s + d) % SUBJ, cov))
        SR[k, s] = total

    both = (0, 1)
    both = (0, 1)
    for i, (h, first_block, blocks) in enumerate(CHUNKS):
        chunks[i].wait()
        if i + AHEAD < len(chunks):
            chunks[i + AHEAD].start()
        elif i + AHEAD == len(chunks):
            for copy in small[1:]:
                copy.start()
        predict(h, first_block, blocks)
        if i == 0:
            pl.semaphore_wait(barrier, len(peers))
        for at in range(first_block // EIGHTH, (first_block + blocks) // EIGHTH):
            part, d = at // 2, at % 2
            rs_far(h, 0, part, d)
            rs_near(h, 0, part, d)
            rs_far(h, 1, part, d)
    for h in both:
        rs_on(h, 0, 0)
    for h in both:
        for d in both:
            rs_near(h, 1, 0, d)
    for h in both:
        rs_on(h, 0, 1)
    for h in both:
        for d in both:
            rs_near(h, 1, 1, d)
    for h in both:
        rs_on(h, 1, 0)
    for h in both:
        rs_second(h, 0, 0)
    for h in both:
        rs_on(h, 1, 1)
    for h in both:
        rs_second(h, 0, 1)
    for h in both:
        rs_second(h, 1, 0)
    for h in both:
        rs_second(h, 1, 1)
    prepare()
    for k in both:
        for h in both:
            rs_end(h, k)
        scan_a(k)
    for k in both:
        scan_a_local(k)
    for k in both:
        scan_b(k)
    for k in both:
        scan_b_local(k)
    for k in both:
        scan_c(k)
        for part in both:
            for h in both:
                ag_first(h, k, part)
    for step in (ag_second, ag_third):
        for k in both:
            for part in both:
                for h in both:
                    step(h, k, part)
    for k in both:
        total = jnp.zeros((PATHS // 2, COLS), F32)
        for part in both:
            for h in both:
                ag_end(h, k, part)
            total = score(k, part, total)
        score_out(k, total)

    def convert(block, carry):
        lanes = pl.ds(pl.multiple_of(block * LANES, LANES), LANES)
        for g in range(4):
            weights_out[g * 8 : g * 8 + 8, lanes] = W[
                pl.ds(g * 8 * BLOCKS + block, 8, stride=BLOCKS), :
            ]
        return carry

    lax.fori_loop(0, BLOCKS, convert, 0, unroll=8)
    eye = (
        lax.broadcasted_iota(jnp.int32, (PATHS, PATHS), 0)
        == lax.broadcasted_iota(jnp.int32, (PATHS, PATHS), 1)
    )
    limit = jnp.sum(
        jnp.where(eye, jnp.broadcast_to(PEN[...], (PATHS, PATHS)), 0.0), axis=1, keepdims=True
    )
    wide = C[...].astype(F32)
    for k in both:
        received("s", k)
        total = SR[k, 0]
        for i in range(1, SUBJ):
            total = total + SR[k, i]
        for c in range(2):
            SUM[c, pl.ds(k, PATHS // 2, stride=2), :] = total[:, c * LANES : (c + 1) * LANES]
    scale = 0.1 / jnp.sqrt(F32(SUBJ * ROWS))
    for c in range(2):
        cols = slice(c * LANES, (c + 1) * LANES)
        shifted = wide[:, cols] + scale * SUM[c, 0:PATHS, :]
        sign = jnp.where(shifted > 0, 1.0, jnp.where(shifted < 0, -1.0, 0.0))
        new_out[:, cols] = sign * jnp.maximum(jnp.abs(shifted) - limit, 0.0)
    left_rows = sent_rows[0]
    span = D.at[pl.ds(0, left_rows), :]
    pltpu.make_async_copy(span, span, send_sem.at[0]).wait()


def hand_over(new, weights, new_out, weights_out, sem):
    copies = [pltpu.make_async_copy(new, new_out, sem.at[4])]
    for c in range(4):
        rows = pl.ds(c * 8, 8)
        copies.append(pltpu.make_async_copy(weights.at[rows], weights_out.at[rows], sem.at[c]))
    for copy in copies:
        copy.start()
    for copy in copies:
        copy.wait()


def local(design, coefs, penalty, censor, codes, tie_first, tie_last):
    square = (BLOCKS, LANES)
    vmem = pltpu.VMEM
    dma = pltpu.SemaphoreType.DMA
    new, weights = pl.pallas_call(
        kernel,
        out_shape=(
            jax.ShapeDtypeStruct((PATHS, COLS), F32),
            jax.ShapeDtypeStruct((PATHS, ROWS), F32),
        ),
        in_specs=[pl.BlockSpec(memory_space=pltpu.HBM)] * 7,
        out_specs=(pl.BlockSpec(memory_space=pltpu.VMEM), pl.BlockSpec(memory_space=pltpu.VMEM)),
        scratch_shapes=[
            vmem((ROWS, COLS), BF16),
            vmem((PATHS, COLS), BF16),
            vmem((1, PATHS), F32),
            vmem(square, F32),
            vmem(square, jnp.int32),
            vmem(square, jnp.int32),
            vmem(square, jnp.int32),
            vmem(square, F32),
            vmem((PATHS * BLOCKS + BLOCKS, LANES), F32),
            vmem((2, NBATCH, 2, 2, RING, EIGHTH, LANES), F32),
            vmem((2, NBATCH, 2, RING, HALF, LANES), F32),
            vmem((2, NBATCH, RING, HALF, LANES), F32),
            vmem((2, NBATCH, 3, HALF, LANES), F32),
            vmem((NBATCH, BLOCKS, LANES), F32),
            vmem((NBATCH, BLOCKS, LANES), F32),
            vmem((NBATCH, BLOCKS, LANES), F32),
            vmem((NBATCH, BLOCKS, LANES), F32),
            vmem((NBATCH, 2, 2, 8, LANES), F32),
            vmem((NBATCH, 2, SUBJ, 2, 8, LANES), F32),
            vmem((PATHS * BLOCKS + 2 * BLOCKS, LANES), F32),
            vmem((NBATCH, PATHS // 2, COLS), F32),
            vmem((NBATCH, SUBJ, PATHS // 2, COLS), F32),
            vmem((2, PATHS + 8, LANES), F32),
            dma((len(CHUNKS) + 6,)),
            dma((1,)),
            dma((50,)),
        ],
        compiler_params=pltpu.CompilerParams(
            collective_id=0, has_side_effects=True, vmem_limit_bytes=48 * 2**20
        ),
        cost_estimate=pl.CostEstimate(
            flops=4 * PATHS * ROWS * COLS,
            bytes_accessed=2 * ROWS * COLS + 4 * PATHS * ROWS,
            transcendentals=2 * ROWS,
        ),
    )(
        *(
            pltpu.with_memory_space_constraint(a, pltpu.HBM)
            for a in (
                design,
                coefs.T,
                penalty.reshape(1, PATHS),
                censor.reshape(square),
                codes.reshape(square),
                tie_first.reshape(square),
                tie_last.reshape(square),
            )
        )
    )
    new, weights = pl.pallas_call(
        hand_over,
        out_shape=(
            jax.ShapeDtypeStruct((PATHS, COLS), F32),
            jax.ShapeDtypeStruct((PATHS, ROWS), F32),
        ),
        in_specs=[pl.BlockSpec(memory_space=pltpu.VMEM)] * 2,
        out_specs=(pl.BlockSpec(memory_space=pltpu.HBM), pl.BlockSpec(memory_space=pltpu.HBM)),
        scratch_shapes=[dma((5,))],
        compiler_params=pltpu.CompilerParams(vmem_limit_bytes=40 * 2**20),
    )(new, weights)
    return new.T, weights


def solution(mesh):
    in_specs = (P("subj", "cov"), P("cov", None), P(), P("subj"), P("subj"), P("subj"), P("subj"))
    out_specs = (P("cov", None), P(None, "subj"))
    return jax.shard_map(local, mesh=mesh, in_specs=in_specs, out_specs=out_specs, check_vma=False)
```
